512 devices in a mesh: gx: 32 (over y, x), gy: 16 (over z, core).
Axes of the slice: x: 4, y: 8, z: 8, core: 2. Of those that a mesh axis runs over, the one named last changes fastest.
Arguments:
- probes: bfloat16 [16, 2, 12, 256, 4096], P(None, None, None, 'gx', 'gy'), may hold values from -120 to 120
- material: int32 [12, 256, 4096], P(None, 'gx', 'gy'), may hold values from 0 to 3
- visc_table: float32 [4], replicated, may hold values from 0.5 to 2
- brink_table: float32 [4], replicated, may hold values from 0.1 to 10
- cond_table: float32 [4], replicated, may hold values from 0.5 to 2
- base_flow: float32 [12, 256, 4096], P(None, 'gx', 'gy'), may hold values from 0 to 1
Outputs:
- basis: float32 [16, 2, 12, 256, 4096], P(None, None, None, 'gx', 'gy')
- r_factor: float32 [16, 16], replicated
The draws below stay inside these ranges and needn't reach their ends.
All inputs are finite; a program needn't handle non-finite values.
Results may differ from the reference program's by a relative error of at most 0.0003.
Values may be sent and summed in bfloat16 or wider, within the bound.
No kernel may reach another device: no remote copies, remote signals or barrier semaphores. Data moves between devices by JAX's collectives and lax.ppermute only.
A program may use at most 64 MiB of HBM per device.

```python
import math
import jax
import jax.numpy as jnp
from jax import lax

PROBES = 16
MATS = 4
NZ = 12
NX = 256
NY = 4096
ROWS = 25165824


def draw_probes(key, part):
    key = jax.random.fold_in(key, 11)
    key_base, key_cols = jax.random.split(key, 2)
    shape = (PROBES, 2, NZ, NX, NY)
    col_scale = jnp.exp(jax.random.uniform(key_cols, (PROBES, 1, 1, 1, 1), jnp.float32) * math.log(10.0))
    x_scale = 1.0 + 2.0 * jnp.arange(NX, dtype=jnp.float32).reshape(1, 1, 1, NX, 1) / max(NX - 1, 1)
    base = jnp.clip(jax.random.normal(key_base, shape, jnp.float32), -4.0, 4.0)
    return (base * col_scale * x_scale).astype(jnp.bfloat16)


def plant(result, rng, smallest, high):
    index_at = [jax.random.randint(jax.random.fold_in(rng, axis), (), 0, length) for axis, length in enumerate(result.shape)]
    main_axis = result.shape.index(max(result.shape))
    next_to = index_at[:main_axis] + [(index_at[main_axis] + 1) % result.shape[main_axis]] + index_at[main_axis + 1:]
    return result.at[tuple(index_at)].set(smallest).at[tuple(next_to)].set(high)


def block_levels(stream_key, extent, pieces, smallest, high):
    def one(dim, parts):
        heights = jax.random.uniform(jax.random.fold_in(jax.random.fold_in(stream_key, 6), dim), (parts,), jnp.float32, smallest / len(pieces), high / len(pieces))
        return jnp.repeat(jnp.exp(heights), extent[dim] // parts).reshape((-1,) + (1,) * (len(extent) - dim - 1))

    loudness = one(*pieces[0])
    for cut in pieces[1:]:
        loudness = loudness * one(*cut)
    return loudness


def setup_inputs(seed: int = 0) -> dict:
    streams_of = jax.random.split(jax.random.key(seed), 7)
    probes = draw_probes(jax.random.fold_in(streams_of[6], 71), 0)
    material = plant(jax.random.randint(streams_of[1], (NZ, NX, NY), 0, MATS), jax.random.fold_in(streams_of[1], 1), 0, MATS - 1).astype(jnp.int32)
    visc_table = jnp.clip(jnp.exp(jax.random.uniform(streams_of[2], (MATS,), jnp.float32, math.log(0.5), math.log(2.0))), 0.5, 2.0)
    brink_table = jnp.clip(jnp.exp(jax.random.uniform(streams_of[3], (MATS,), jnp.float32, math.log(0.1), math.log(10.0))), 0.1, 10.0)
    cond_table = jnp.clip(jnp.exp(jax.random.uniform(streams_of[4], (MATS,), jnp.float32, math.log(0.5), math.log(2.0))), 0.5, 2.0)
    base_flow = jnp.clip(1.0 * jax.random.uniform(streams_of[5], (NZ, NX, NY), jnp.float32) ** block_levels(streams_of[5], (NZ, NX, NY), ((1, 32), (2, 16)), -0.2, 0.2), 0.0, 1.0)
    return {"probes": probes, "material": material, "visc_table": visc_table, "brink_table": brink_table, "cond_table": cond_table, "base_flow": base_flow}


def cell_values(material, table):
    total = jnp.zeros(material.shape, jnp.float32)
    for index in range(table.shape[0]):
        total = total + jnp.where(material == index, table[index], jnp.float32(0.0))
    return total

def lap_parts(field):
    center = field[:, :, 1:-1, 1:-1]
    vertical = jnp.pad(center, ((0, 0), (1, 1), (0, 0), (0, 0)))
    beside = field[:, :, 2:, 1:-1] + field[:, :, :-2, 1:-1] + field[:, :, 1:-1, 2:] + field[:, :, 1:-1, :-2]
    beside = beside + vertical[:, 2:] + vertical[:, :-2]
    return (center, 6.0 * center - beside, vertical[:, :-2])

def apply_operator(padded, material, visc_table, brink_table, cond_table, base_flow):
    wide = padded.astype(jnp.float32)
    w_center, w_lap, w_below = lap_parts(wide[:, 0])
    t_center, t_lap, t_below = lap_parts(wide[:, 1])
    visc = cell_values(material, visc_table)
    brink = cell_values(material, brink_table)
    cond = cell_values(material, cond_table)
    image_w = visc * w_lap + brink * w_center - t_center
    image_t = cond * t_lap + 0.5 * w_center + base_flow * (t_center - t_below)
    return jnp.stack([image_w, image_t], axis=1)

def reference(probes, material, visc_table, brink_table, cond_table, base_flow):

    def one_probe(column):
        padded = jnp.pad(column, ((0, 0), (0, 0), (1, 1), (1, 1)))
        return apply_operator(padded[None], material, visc_table, brink_table, cond_table, base_flow)[0]
    image = lax.map(one_probe, probes)
    flat = image.reshape(image.shape[0], -1)
    gram = jnp.dot(flat, flat.T, precision=lax.Precision.HIGHEST)
    upper = jnp.linalg.cholesky(gram).T
    solved = jax.scipy.linalg.solve_triangular(upper.T, flat, lower=True)
    scale = math.sqrt(ROWS)
    basis = (solved * scale).reshape(image.shape)
    return (basis, upper / scale)
```

```python
import functools
import math

import jax
import jax.numpy as jnp
from jax import lax
from jax.experimental import pallas as pl
from jax.experimental.pallas import tpu as pltpu
from jax.sharding import PartitionSpec as P

PROBES = 16
SLABS = 24
DEPTH = 12
XS = 8
YS = 256
BLOCK = PROBES * XS
F32 = jnp.float32
BF16 = jnp.bfloat16
NT = (((1,), (1,)), ((), ()))
TN = (((0,), (0,)), ((), ()))


def iota(shape, dim):
    return lax.broadcasted_iota(jnp.int32, shape, dim)


def params():
    return pltpu.CompilerParams(vmem_limit_bytes=24 * 1024 * 1024)


def pick(material, table):
    value = jnp.where(material == 0, table[0], table[1])
    value = jnp.where(material == 2, table[2], value)
    return jnp.where(material == 3, table[3], value)


def faces_kernel(probes, x_low, x_high, y_low, y_high, wide):
    field = probes[...].astype(F32).transpose(1, 0, 2, 3).reshape(SLABS * BLOCK, YS)
    wide[0] = field[:, :128]
    wide[1] = field[:, 128:]
    for face, row in ((x_low, 0), (x_high, XS - 1)):
        for half in range(2):
            rows = wide[half, pl.ds(row, SLABS * PROBES, stride=XS), :]
            face[:, half * 128 : half * 128 + 128] = rows.astype(BF16)
    row, lane = iota((16, YS), 0), iota((16, YS), 1)
    ends = (lane == jnp.where(row == 0, 0, YS - 1)) & (row < 2)
    sides = lax.dot_general(ends.astype(BF16), field.astype(BF16), NT, preferred_element_type=F32)
    y_low[...] = sides[0:1]
    y_high[...] = sides[1:2]


def faces(probes):
    return pl.pallas_call(
        faces_kernel,
        out_shape=[jax.ShapeDtypeStruct((SLABS * PROBES, YS), BF16)] * 2
        + [jax.ShapeDtypeStruct((1, SLABS * BLOCK), F32)] * 2,
        scratch_shapes=[pltpu.VMEM((2, SLABS * BLOCK, 128), F32)],
        compiler_params=params(),
        name="faces",
    )(probes)


def inner_kernel(probes, material, flow, visc_table, brink_table, cond_table, image, visc, brink, cond):
    kind = material[...]
    visc[...] = pick(kind, visc_table)
    brink[...] = pick(kind, brink_table)
    cond[...] = pick(kind, cond_table)
    row, lane = iota((YS, YS), 0), iota((YS, YS), 1)
    along_y = jnp.where(row == lane, 6.0, jnp.where(jnp.abs(row - lane) == 1, -1.0, 0.0)).astype(BF16)
    rows = SLABS * XS
    row, lane = iota((rows, rows), 0), iota((rows, rows), 1)
    along_x = jnp.where((jnp.abs(row - lane) == 1) & (row // XS == lane // XS), -1.0, 0.0).astype(BF16)

    def step(probe, carry):
        wide = probes[probe].astype(F32)
        packed = wide.reshape(rows, YS).astype(BF16)
        lap = jnp.dot(packed, along_y, preferred_element_type=F32)
        lap = lap + jnp.dot(along_x, packed, preferred_element_type=F32)
        lap = lap.reshape(SLABS, XS, YS)
        none = jnp.zeros((1, XS, YS), F32)

        def vertical(field):
            below = jnp.concatenate([none, field[:-1]], axis=0)
            above = jnp.concatenate([field[1:], none], axis=0)
            return below, above

        w, t = wide[:DEPTH], wide[DEPTH:]
        w_below, w_above = vertical(w)
        t_below, t_above = vertical(t)
        w_lap = lap[:DEPTH] - (w_below + w_above)
        t_lap = lap[DEPTH:] - (t_below + t_above)
        image[probe, :DEPTH] = visc[...] * w_lap + brink[...] * w - t
        image[probe, DEPTH:] = cond[...] * t_lap + 0.5 * w + flow[...] * (t - t_below)
        return carry

    lax.fori_loop(0, PROBES, step, 0)


def inner(probes, material, flow, tables):
    whole = pl.BlockSpec(memory_space=pltpu.VMEM)
    small = pl.BlockSpec(memory_space=pltpu.SMEM)
    cells = (DEPTH, XS, YS)
    return pl.pallas_call(
        inner_kernel,
        out_shape=pltpu.VMEM((PROBES, SLABS, XS, YS), F32),
        in_specs=[whole, whole, whole, small, small, small],
        out_specs=whole,
        scratch_shapes=[pltpu.VMEM(cells, F32)] * 3,
        compiler_params=params(),
        cost_estimate=pl.CostEstimate(flops=800_000_000, bytes_accessed=5_000_000, transcendentals=0),
        name="inner",
    )(probes, material, flow, *tables)


def gram_kernel(image, x_low, x_high, y_low, y_high, material, visc_table, cond_table, parts, gram, total):
    row, lane = iota((BLOCK, 2 * PROBES), 0), iota((BLOCK, 2 * PROBES), 1)
    at_low = (row % XS == 0) & (lane == row // XS)
    at_high = (row % XS == XS - 1) & (lane == row // XS + PROBES)
    place = jnp.where(at_low | at_high, 1.0, 0.0).astype(BF16)
    row, lane = iota((16, YS), 0), iota((16, YS), 1)
    ends = ((lane == jnp.where(row == 0, 0, YS - 1)) & (row < 2)).astype(BF16)
    side = iota((16, BLOCK), 0)
    for slab in range(SLABS):
        table = visc_table if slab < DEPTH else cond_table
        factor = pick(material[slab % DEPTH], table)
        span = pl.ds(slab * PROBES, PROBES)
        edges = jnp.concatenate([x_low[span, :], x_high[span, :]], axis=0)
        halo = jnp.dot(place, edges, preferred_element_type=F32)
        cells = pl.ds(slab * BLOCK, BLOCK)
        columns = jnp.where(side == 0, y_low[:, cells], jnp.where(side == 1, y_high[:, cells], 0.0))
        halo = halo + lax.dot_general(columns.astype(BF16), ends, TN, preferred_element_type=F32)
        full = image[:, slab] - factor[None] * halo.reshape(PROBES, XS, YS)
        full = full.reshape(BLOCK, YS)
        high = full.astype(BF16)
        low = (full - high.astype(F32)).astype(BF16)
        both = jnp.concatenate([high, low], axis=0)
        parts[slab] = both
        product = lax.dot_general(both, both, NT, preferred_element_type=F32)
        if slab == 0:
            total[...] = product
        else:
            total[...] += product
    square = total[:BLOCK, :BLOCK] + total[BLOCK:, :BLOCK] + total[:BLOCK, BLOCK:] + total[BLOCK:, BLOCK:]
    row, lane = iota((BLOCK, BLOCK), 0), iota((BLOCK, BLOCK), 1)
    square = jnp.where(row % XS == lane % XS, square, 0.0)
    square = jnp.sum(square.reshape(PROBES, XS, BLOCK), axis=1)
    top, bottom = square[:8], square[8:]
    first = iota((8, BLOCK), 1) % XS < XS // 2
    top = top + pltpu.roll(top, BLOCK - XS // 2, 1)
    bottom = bottom + pltpu.roll(bottom, XS // 2, 1)
    gram[...] = jnp.where(first, top, bottom)


def gram(image, halos, material, visc_table, cond_table):
    whole = pl.BlockSpec(memory_space=pltpu.VMEM)
    small = pl.BlockSpec(memory_space=pltpu.SMEM)
    return pl.pallas_call(
        gram_kernel,
        out_shape=[
            pltpu.VMEM((SLABS, 2 * BLOCK, YS), BF16),
            jax.ShapeDtypeStruct((8, BLOCK), F32),
        ],
        in_specs=[whole] * 6 + [small] * 2,
        out_specs=[whole] * 2,
        scratch_shapes=[pltpu.VMEM((2 * BLOCK, 2 * BLOCK), F32)],
        compiler_params=params(),
        name="gram",
    )(image, *halos, material, visc_table, cond_table)


CHUNK = 4


def basis_kernel(scale, parts, pieces, basis, factor, result, sems):
    shape = (PROBES, BLOCK)
    row, lane = iota(shape, 0), iota(shape, 1)
    half = jnp.sum(pieces[...], axis=0)
    lane8 = iota((8, BLOCK), 1)
    for step in (1, 2):
        ahead = pltpu.roll(half, BLOCK - step, 1)
        behind = pltpu.roll(half, step, 1)
        half = half + jnp.where(lane8 & step == 0, ahead, behind)
    first = lane8 % XS < XS // 2
    top = jnp.where(first, half, pltpu.roll(half, XS // 2, 1))
    bottom = jnp.where(first, pltpu.roll(half, BLOCK - XS // 2, 1), half)
    left = jnp.concatenate([top, bottom], axis=0)
    right = jnp.where(lane // XS == row, 1.0, 0.0).astype(F32)
    pivots = jnp.ones(shape, F32)
    for k in range(PROBES):
        column = jnp.broadcast_to(left[:, k * XS : k * XS + 1], shape)
        pivot = jnp.broadcast_to(column[k : k + 1], shape)
        pivots = jnp.where(row == k, pivot, pivots)
        if k + 1 < PROBES:
            ratio = jnp.where(row > k, column / pivot, 0.0)
            left = left - ratio * jnp.broadcast_to(left[k : k + 1], shape)
            right = right - ratio * jnp.broadcast_to(right[k : k + 1], shape)
    root = lax.rsqrt(pivots)
    root = root * (1.5 - 0.5 * pivots * root * root)
    right = right * (root * scale)
    mask = jnp.where(iota((XS, BLOCK), 1) % XS == iota((XS, BLOCK), 0), 1.0, 0.0)
    weight = jnp.concatenate([mask * right[q : q + 1] for q in range(PROBES)], axis=0)
    high = weight.astype(BF16)
    low = (weight - high.astype(F32)).astype(BF16)
    weight = jnp.concatenate(
        [jnp.concatenate([high, high], axis=1), jnp.concatenate([low, low], axis=1)], axis=0
    )

    copies = []
    for slab in range(SLABS):
        out = jnp.dot(weight, parts[slab], preferred_element_type=F32)
        out = out[:BLOCK] + out[BLOCK:]
        result[:, slab] = out.reshape(PROBES, XS, YS)
        if slab % CHUNK == CHUNK - 1:
            span = pl.ds(slab - CHUNK + 1, CHUNK)
            copy = pltpu.make_async_copy(result.at[:, span], basis.at[:, span], sems.at[slab // CHUNK])
            copy.start()
            copies.append(copy)
    upper = jnp.where(lane // XS >= row, left * (root * (1.0 / scale)), 0.0)
    chosen = jnp.where(iota((BLOCK, PROBES), 0) == XS * iota((BLOCK, PROBES), 1), 1.0, 0.0)
    factor[...] = jnp.dot(upper, chosen, precision=lax.Precision.HIGHEST, preferred_element_type=F32)
    for copy in copies:
        copy.wait()


def orthonormal(parts, pieces, scale):
    whole = pl.BlockSpec(memory_space=pltpu.VMEM)
    return pl.pallas_call(
        functools.partial(basis_kernel, scale),
        out_shape=[
            jax.ShapeDtypeStruct((PROBES, SLABS, XS, YS), F32),
            jax.ShapeDtypeStruct((PROBES, PROBES), F32),
        ],
        in_specs=[whole, whole],
        out_specs=[pl.BlockSpec(memory_space=pl.ANY), whole],
        scratch_shapes=[
            pltpu.VMEM((PROBES, SLABS, XS, YS), F32),
            pltpu.SemaphoreType.DMA((SLABS // CHUNK,)),
        ],
        compiler_params=params(),
        name="orthonormal",
    )(parts, pieces)


def shift(array, axis, by):
    count = lax.axis_size(axis)
    return lax.ppermute(array, axis, [(i, i + by) for i in range(count) if 0 <= i + by < count])


def all_copies(array, axis):
    copies = jnp.broadcast_to(array[None], (lax.axis_size(axis),) + array.shape)
    return lax.all_to_all(copies, axis, 0, 0)


def on_device(probes, material, visc_table, brink_table, cond_table, base_flow):
    shape = probes.shape
    probes = probes.reshape(PROBES, SLABS, XS, YS)
    x_low, x_high, y_low, y_high = faces(probes)
    halos = (shift(x_high, "gx", 1), shift(x_low, "gx", -1), shift(y_high, "gy", 1), shift(y_low, "gy", -1))
    image = inner(probes, material, base_flow, (visc_table, brink_table, cond_table))
    parts, local = gram(image, halos, material, visc_table, cond_table)
    slab_sum = jnp.sum(all_copies(local, "gy"), axis=0)
    pieces = all_copies(slab_sum, "gx")
    rows_total = SLABS * XS * YS * lax.axis_size("gx") * lax.axis_size("gy")
    basis, factor = orthonormal(parts, pieces, math.sqrt(rows_total))
    return (basis.reshape(shape), factor)


def solution(mesh):
    grid = P(None, "gx", "gy")
    in_specs = (P(None, None, None, "gx", "gy"), grid, P(), P(), P(), grid)
    out_specs = (P(None, None, None, "gx", "gy"), P())
    return jax.shard_map(
        on_device, mesh=mesh, in_specs=in_specs, out_specs=out_specs, check_vma=False
    )
```

```python
import functools
import math

import jax
import jax.numpy as jnp
from jax import lax
from jax.experimental import pallas as pl
from jax.experimental.pallas import tpu as pltpu
from jax.sharding import PartitionSpec as P

PROBES = 16
SLABS = 24
DEPTH = 12
XS = 8
YS = 256
BLOCK = PROBES * XS
F32 = jnp.float32
BF16 = jnp.bfloat16
NT = (((1,), (1,)), ((), ()))
TN = (((0,), (0,)), ((), ()))


def iota(shape, dim):
    return lax.broadcasted_iota(jnp.int32, shape, dim)


def params():
    return pltpu.CompilerParams(vmem_limit_bytes=24 * 1024 * 1024)


def pick(material, table):
    value = jnp.where(material == 0, table[0], table[1])
    value = jnp.where(material == 2, table[2], value)
    return jnp.where(material == 3, table[3], value)


def first_ends(parity):
    return (XS - 1) * (1 - parity[0]), (YS - 1) * (1 - parity[1])


def parities():
    return lax.axis_index("gx") % 2, lax.axis_index("gy") % 2


LOADS = 4


def whole_rows(wide, slab):
    return jnp.concatenate([wide[0, slab], wide[1, slab]], axis=1)


def faces_kernel(
    probes, material, flow_in, visc_in, brink_in, cond_in,
    x_first, x_second, y_first, y_second, wide, flow, visc, brink, cond,
    packed, kind, visc_table, brink_table, cond_table, sems,
):
    each = PROBES // LOADS
    loads = [
        pltpu.make_async_copy(probes.at[pl.ds(i * each, each)], packed.at[pl.ds(i * each, each)], sems.at[i])
        for i in range(LOADS)
    ]
    others = ((material, kind), (visc_in, visc_table), (brink_in, brink_table), (cond_in, cond_table), (flow_in, flow))
    others = [pltpu.make_async_copy(src, dst, sems.at[LOADS + i]) for i, (src, dst) in enumerate(others)]
    for copy in loads + others:
        copy.start()
    x_end, y_end = first_ends(parities())
    for i, copy in enumerate(loads):
        copy.wait()
        for probe in range(i * each, (i + 1) * each):
            field = packed[probe].astype(F32)
            for half in range(2):
                wide[half, :, probe * XS : (probe + 1) * XS, :] = field[:, :, half * 128 : half * 128 + 128]
    rows = wide.reshape(2, SLABS * BLOCK, 128)
    for face, end in ((x_first, x_end), (x_second, XS - 1 - x_end)):
        for half in range(2):
            ends = rows[half, pl.ds(end, SLABS * PROBES, stride=XS), :]
            face[:, half * 128 : half * 128 + 128] = ends.astype(BF16)
    lane = iota((BLOCK, 128), 1)
    sides = jnp.zeros((BLOCK, 128), F32)
    for slab in range(SLABS):
        sides = jnp.where(lane == slab, pltpu.roll(wide[0, slab], slab, 1), sides)
        sides = jnp.where(lane == slab + 32, pltpu.roll(wide[1, slab], slab + 33, 1), sides)
    sides = sides.T
    low, high = sides[:32], sides[32:64]
    y_first[...] = jnp.where(y_end == 0, low, high).astype(BF16)
    y_second[...] = jnp.where(y_end == 0, high, low).astype(BF16)
    for copy in others:
        copy.wait()
    visc[...] = pick(kind[...], visc_table)
    brink[...] = pick(kind[...], brink_table)
    cond[...] = pick(kind[...], cond_table)


def faces(probes, material, flow, tables):
    cells = (DEPTH, XS, YS)
    arrays = [pltpu.with_memory_space_constraint(a, pltpu.HBM) for a in (probes, material, flow, *tables)]
    whole = pl.BlockSpec(memory_space=pltpu.VMEM)
    return pl.pallas_call(
        faces_kernel,
        out_shape=[jax.ShapeDtypeStruct((SLABS * PROBES, YS), BF16)] * 2
        + [jax.ShapeDtypeStruct((32, BLOCK), BF16)] * 2
        + [pltpu.VMEM((2, SLABS, BLOCK, 128), F32)]
        + [pltpu.VMEM(cells, F32)] * 4,
        in_specs=[pl.BlockSpec(memory_space=pl.ANY)] * 6,
        out_specs=[whole] * 9,
        scratch_shapes=[
            pltpu.VMEM((PROBES, SLABS, XS, YS), BF16),
            pltpu.VMEM(cells, jnp.int32),
            pltpu.SMEM((4,), F32),
            pltpu.SMEM((4,), F32),
            pltpu.SMEM((4,), F32),
            pltpu.SemaphoreType.DMA((LOADS + 5,)),
        ],
        compiler_params=params(),
        name="faces",
    )(*arrays)


def inner_kernel(wide, flow, visc, brink, cond, image):
    row, lane = iota((YS, YS), 0), iota((YS, YS), 1)
    along_y = jnp.where(row == lane, 6.0, jnp.where(jnp.abs(row - lane) == 1, -1.0, 0.0)).astype(BF16)
    along_x = jnp.where((jnp.abs(row - lane) == 1) & (row // XS == lane // XS), -1.0, 0.0).astype(BF16)
    block = (PROBES, XS, YS)

    def around(z):
        if z == 0:
            return whole_rows(wide, 1)
        if z == DEPTH - 1:
            return whole_rows(wide, z - 1)
        return whole_rows(wide, z - 1) + whole_rows(wide, z + 1)

    def around_t(z):
        if z == 0:
            return whole_rows(wide, DEPTH + 1)
        if z == DEPTH - 1:
            return whole_rows(wide, DEPTH + z - 1)
        return whole_rows(wide, DEPTH + z - 1) + whole_rows(wide, DEPTH + z + 1)

    for z in range(DEPTH):
        w, t = whole_rows(wide, z), whole_rows(wide, DEPTH + z)
        both = jnp.concatenate([w.astype(BF16), t.astype(BF16)], axis=0)
        lap = jnp.dot(both, along_y, preferred_element_type=F32)
        lap = lap + jnp.dot(along_x, both, preferred_element_type=F32)
        w_lap = (lap[:BLOCK] - around(z)).reshape(block)
        t_lap = (lap[BLOCK:] - around_t(z)).reshape(block)
        w3, t3 = w.reshape(block), t.reshape(block)
        rise = t3 if z == 0 else t3 - whole_rows(wide, DEPTH + z - 1).reshape(block)
        image[z] = (visc[z][None] * w_lap + brink[z][None] * w3 - t3).reshape(BLOCK, YS)
        image[DEPTH + z] = (cond[z][None] * t_lap + 0.5 * w3 + flow[z][None] * rise).reshape(BLOCK, YS)


def inner(wide, flow, visc, brink, cond):
    whole = pl.BlockSpec(memory_space=pltpu.VMEM)
    return pl.pallas_call(
        inner_kernel,
        out_shape=pltpu.VMEM((SLABS, BLOCK, YS), F32),
        in_specs=[whole] * 5,
        out_specs=whole,
        compiler_params=params(),
        cost_estimate=pl.CostEstimate(flops=800_000_000, bytes_accessed=6_000_000, transcendentals=0),
        name="inner",
    )(wide, flow, visc, brink, cond)


def gram_kernel(image, visc, cond, x_first, x_second, y_first, y_second, parts, gram, total):
    x_end, y_end = first_ends(parities())
    row, lane = iota((BLOCK, 2 * PROBES), 0), iota((BLOCK, 2 * PROBES), 1)
    target = jnp.where(lane < PROBES, x_end, XS - 1 - x_end)
    place = jnp.where((row % XS == target) & (row // XS == lane % PROBES), 1.0, 0.0).astype(BF16)
    columns = jnp.concatenate([y_first[...].astype(F32), y_second[...].astype(F32)], axis=0).T
    place = jnp.concatenate([place, columns.astype(BF16)], axis=1)
    row, lane = iota((64, YS), 0), iota((64, YS), 1)
    at_end = jnp.where(row < 32, y_end, YS - 1 - y_end) == lane
    for slab in range(SLABS):
        factor = visc[slab] if slab < DEPTH else cond[slab - DEPTH]
        span = pl.ds(slab * PROBES, PROBES)
        ends = jnp.where(at_end & (row % 32 == slab), 1.0, 0.0).astype(BF16)
        edges = jnp.concatenate([x_first[span, :], x_second[span, :], ends], axis=0)
        halo = jnp.dot(place, edges, preferred_element_type=F32).reshape(PROBES, XS, YS)
        full = image[slab] - (factor[None] * halo).reshape(BLOCK, YS)
        high = full.astype(BF16)
        parts[slab, :BLOCK] = high
        parts[slab, BLOCK:] = (full - high.astype(F32)).astype(BF16)
    for slab in range(SLABS):
        product = lax.dot_general(parts[slab], parts[slab, :BLOCK], NT, preferred_element_type=F32)
        if slab == 0:
            total[...] = product
        else:
            total[...] += product
    mixed = total[BLOCK:]
    square = total[:BLOCK] + mixed + mixed.T
    row, lane = iota((BLOCK, BLOCK), 0), iota((BLOCK, BLOCK), 1)
    square = jnp.where(row % XS == lane % XS, square, 0.0)
    square = jnp.sum(square.reshape(PROBES, XS, BLOCK), axis=1)
    top, bottom = square[:8], square[8:]
    first = iota((8, BLOCK), 1) % XS < XS // 2
    top = top + pltpu.roll(top, BLOCK - XS // 2, 1)
    bottom = bottom + pltpu.roll(bottom, XS // 2, 1)
    gram[...] = jnp.where(first, top, bottom)


def gram(image, visc, cond, halos):
    whole = pl.BlockSpec(memory_space=pltpu.VMEM)
    return pl.pallas_call(
        gram_kernel,
        out_shape=[
            pltpu.VMEM((SLABS, 2 * BLOCK, YS), BF16),
            jax.ShapeDtypeStruct((8, BLOCK), F32),
        ],
        in_specs=[whole] * 7,
        out_specs=[whole] * 2,
        scratch_shapes=[pltpu.VMEM((2 * BLOCK, BLOCK), F32)],
        compiler_params=params(),
        name="gram",
    )(image, visc, cond, *halos)


CHUNK = 4


def basis_kernel(scale, parts, pieces, basis, factor, result, sems):
    shape = (PROBES, BLOCK)
    row, lane = iota(shape, 0), iota(shape, 1)
    half = jnp.sum(pieces[...], axis=0)
    lane8 = iota((8, BLOCK), 1)
    for step in (1, 2):
        ahead = pltpu.roll(half, BLOCK - step, 1)
        behind = pltpu.roll(half, step, 1)
        half = half + jnp.where(lane8 & step == 0, ahead, behind)
    first = lane8 % XS < XS // 2
    top = jnp.where(first, half, pltpu.roll(half, XS // 2, 1))
    bottom = jnp.where(first, pltpu.roll(half, BLOCK - XS // 2, 1), half)
    left = jnp.concatenate([top, bottom], axis=0)
    right = jnp.where(lane // XS == row, 1.0, 0.0).astype(F32)
    heads, crosses, tails = (jnp.ones(shape, F32) for _ in range(3))
    for k in range(0, PROBES, 2):
        one = jnp.broadcast_to(left[:, k * XS : k * XS + 1], shape)
        two = jnp.broadcast_to(left[:, (k + 1) * XS : (k + 1) * XS + 1], shape)
        head = jnp.broadcast_to(one[k : k + 1], shape)
        cross = jnp.broadcast_to(one[k + 1 : k + 2], shape)
        tail = jnp.broadcast_to(two[k + 1 : k + 2], shape)
        mine = row // 2 == k // 2
        heads = jnp.where(mine, head, heads)
        crosses = jnp.where(mine, cross, crosses)
        tails = jnp.where(mine, tail, tails)
        if k + 2 < PROBES:
            over = jnp.where(row > k + 1, 1.0 / (head * tail - cross * cross), 0.0)
            first_ratio = (tail * one - cross * two) * over
            second_ratio = (head * two - cross * one) * over
            left, right = (
                side
                - first_ratio * jnp.broadcast_to(side[k : k + 1], shape)
                - second_ratio * jnp.broadcast_to(side[k + 1 : k + 2], shape)
                for side in (left, right)
            )
    odd = row % 2 == 1
    ratio = jnp.where(odd, crosses / heads, 0.0)
    left, right = (side - ratio * pltpu.roll(side, 1, 0) for side in (left, right))
    pivots = jnp.where(odd, tails - ratio * crosses, heads)
    root = lax.rsqrt(pivots)
    root = root * (1.5 - 0.5 * pivots * root * root)
    right = right * (root * scale)
    mask = jnp.where(iota((XS, BLOCK), 1) % XS == iota((XS, BLOCK), 0), 1.0, 0.0)
    weight = jnp.concatenate([mask * right[q : q + 1] for q in range(PROBES)], axis=0)
    high = weight.astype(BF16)
    low = (weight - high.astype(F32)).astype(BF16)
    weight = jnp.concatenate(
        [jnp.concatenate([high, high], axis=1), jnp.concatenate([low, low], axis=1)], axis=0
    )

    copies = []
    for slab in range(SLABS):
        out = jnp.dot(weight, parts[slab], preferred_element_type=F32)
        out = out[:BLOCK] + out[BLOCK:]
        result[:, slab] = out.reshape(PROBES, XS, YS)
        if slab % CHUNK == CHUNK - 1:
            span = pl.ds(slab - CHUNK + 1, CHUNK)
            copy = pltpu.make_async_copy(result.at[:, span], basis.at[:, span], sems.at[slab // CHUNK])
            copy.start()
            copies.append(copy)
    upper = jnp.where(lane // XS >= row, left * (root * (1.0 / scale)), 0.0)
    chosen = jnp.where(iota((BLOCK, PROBES), 0) == XS * iota((BLOCK, PROBES), 1), 1.0, 0.0)
    factor[...] = jnp.dot(upper, chosen, precision=lax.Precision.HIGHEST, preferred_element_type=F32)
    for copy in copies:
        copy.wait()


def orthonormal(parts, pieces, scale):
    whole = pl.BlockSpec(memory_space=pltpu.VMEM)
    return pl.pallas_call(
        functools.partial(basis_kernel, scale),
        out_shape=[
            jax.ShapeDtypeStruct((PROBES, SLABS, XS, YS), F32),
            jax.ShapeDtypeStruct((PROBES, PROBES), F32),
        ],
        in_specs=[whole, whole],
        out_specs=[pl.BlockSpec(memory_space=pl.ANY), whole],
        scratch_shapes=[
            pltpu.VMEM((PROBES, SLABS, XS, YS), F32),
            pltpu.SemaphoreType.DMA((SLABS // CHUNK,)),
        ],
        compiler_params=params(),
        name="orthonormal",
    )(parts, pieces)


def swap(array, axis, first):
    count = lax.axis_size(axis)
    pairs = [(i, i + 1) for i in range(0 if first else 1, count - 1, 2)]
    return lax.ppermute(array, axis, pairs + [(j, i) for i, j in pairs])


def all_copies(array, axes):
    copies = jnp.broadcast_to(array[None], (lax.axis_size(axes),) + array.shape)
    return lax.all_to_all(copies, axes, 0, 0)


def on_device(probes, material, visc_table, brink_table, cond_table, base_flow):
    shape = probes.shape
    probes = probes.reshape(PROBES, SLABS, XS, YS)
    x_first, x_second, y_first, y_second, wide, flow, visc, brink, cond = faces(
        probes, material, base_flow, (visc_table, brink_table, cond_table)
    )
    halos = (
        swap(x_first, "gx", True),
        swap(x_second, "gx", False),
        swap(y_first, "gy", True),
        swap(y_second, "gy", False),
    )
    image = inner(wide, flow, visc, brink, cond)
    parts, local = gram(image, visc, cond, halos)
    slab_sum = jnp.sum(all_copies(local, "gy"), axis=0)
    pieces = all_copies(slab_sum, "gx")
    rows_total = SLABS * XS * YS * lax.axis_size("gx") * lax.axis_size("gy")
    basis, factor = orthonormal(parts, pieces, math.sqrt(rows_total))
    return (basis.reshape(shape), factor)


def solution(mesh):
    grid = P(None, "gx", "gy")
    in_specs = (P(None, None, None, "gx", "gy"), grid, P(), P(), P(), grid)
    out_specs = (P(None, None, None, "gx", "gy"), P())
    return jax.shard_map(
        on_device, mesh=mesh, in_specs=in_specs, out_specs=out_specs, check_vma=False
    )
```

```python
import functools
import math

import jax
import jax.numpy as jnp
from jax import lax
from jax.experimental import pallas as pl
from jax.experimental.pallas import tpu as pltpu
from jax.sharding import PartitionSpec as P

GX = ("y", "x")
GY = ("z", "core")
PROBES = 16
SLABS = 24
DEPTH = 12
XS = 8
YS = 256
BLOCK = PROBES * XS
F32 = jnp.float32
BF16 = jnp.bfloat16
NT = (((1,), (1,)), ((), ()))
TN = (((0,), (0,)), ((), ()))


def iota(shape, dim):
    return lax.broadcasted_iota(jnp.int32, shape, dim)


def params():
    return pltpu.CompilerParams(vmem_limit_bytes=24 * 1024 * 1024)


def pick(material, table):
    value = jnp.where(material == 0, table[0], table[1])
    value = jnp.where(material == 2, table[2], value)
    return jnp.where(material == 3, table[3], value)


def first_ends(parity):
    return (XS - 1) * (1 - parity[0]), (YS - 1) * (1 - parity[1])


def parities():
    return lax.axis_index(GX) % 2, lax.axis_index(GY) % 2


LOADS = 4


def whole_rows(wide, slab):
    return jnp.concatenate([wide[0, slab], wide[1, slab]], axis=1)


def load_kernel(probes, material, flow_in, visc_in, brink_in, cond_in, x_second, wide, flow, kind, tables, packed, sems):
    each = PROBES // LOADS
    loads = [
        pltpu.make_async_copy(probes.at[pl.ds(i * each, each)], packed.at[pl.ds(i * each, each)], sems.at[i])
        for i in range(LOADS)
    ]
    others = ((material, kind), (visc_in, tables.at[0]), (brink_in, tables.at[1]), (cond_in, tables.at[2]), (flow_in, flow))
    others = [pltpu.make_async_copy(src, dst, sems.at[LOADS + i]) for i, (src, dst) in enumerate(others)]
    for copy in loads + others:
        copy.start()
    for i, copy in enumerate(loads):
        copy.wait()
        for probe in range(i * each, (i + 1) * each):
            field = packed[probe].astype(F32)
            for half in range(2):
                wide[half, :, probe * XS : (probe + 1) * XS, :] = field[:, :, half * 128 : half * 128 + 128]
    x_end, _ = first_ends(parities())
    x_face(wide, XS - 1 - x_end, x_second)
    for copy in others:
        copy.wait()


def x_face(wide, end, face):
    rows = wide.reshape(2, SLABS * BLOCK, 128)
    for half in range(2):
        ends = rows[half, pl.ds(end, SLABS * PROBES, stride=XS), :]
        face[:, half * 128 : half * 128 + 128] = ends.astype(BF16)


def load(probes, material, flow, tables):
    cells = (DEPTH, XS, YS)
    arrays = [pltpu.with_memory_space_constraint(a, pltpu.HBM) for a in (probes, material, flow, *tables)]
    whole = pl.BlockSpec(memory_space=pltpu.VMEM)
    return pl.pallas_call(
        load_kernel,
        out_shape=[
            pltpu.VMEM((SLABS * PROBES, YS), BF16),
            pltpu.VMEM((2, SLABS, BLOCK, 128), F32),
            pltpu.VMEM(cells, F32),
            pltpu.VMEM(cells, jnp.int32),
            pltpu.SMEM((3, 4), F32),
        ],
        in_specs=[pl.BlockSpec(memory_space=pl.ANY)] * 6,
        out_specs=[whole] * 4 + [pl.BlockSpec(memory_space=pltpu.SMEM)],
        scratch_shapes=[
            pltpu.VMEM((PROBES, SLABS, XS, YS), BF16),
            pltpu.SemaphoreType.DMA((LOADS + 5,)),
        ],
        compiler_params=params(),
        name="load",
    )(*arrays)


def faces_kernel(wide, kind, tables, x_first, y_first, y_second, visc, brink, cond):
    x_end, y_end = first_ends(parities())
    x_face(wide, x_end, x_first)
    lane = iota((BLOCK, 128), 1)
    sides = jnp.zeros((BLOCK, 128), F32)
    for slab in range(SLABS):
        sides = jnp.where(lane == slab, pltpu.roll(wide[0, slab], slab, 1), sides)
        sides = jnp.where(lane == slab + 32, pltpu.roll(wide[1, slab], slab + 33, 1), sides)
    sides = sides.T
    low, high = sides[:32], sides[32:64]
    y_first[...] = jnp.where(y_end == 0, low, high).astype(BF16)
    y_second[...] = jnp.where(y_end == 0, high, low).astype(BF16)
    for i, value in enumerate((visc, brink, cond)):
        value[...] = pick(kind[...], [tables[i, j] for j in range(4)])


def faces(wide, kind, tables):
    whole = pl.BlockSpec(memory_space=pltpu.VMEM)
    return pl.pallas_call(
        faces_kernel,
        out_shape=[pltpu.VMEM((SLABS * PROBES, YS), BF16)]
        + [pltpu.VMEM((32, BLOCK), BF16)] * 2
        + [pltpu.VMEM((DEPTH, XS, YS), F32)] * 3,
        in_specs=[whole] * 2 + [pl.BlockSpec(memory_space=pltpu.SMEM)],
        out_specs=[whole] * 6,
        compiler_params=params(),
        name="faces",
    )(wide, kind, tables)


def inner_kernel(wide, flow, visc, brink, cond, image):
    row, lane = iota((YS, YS), 0), iota((YS, YS), 1)
    along_y = jnp.where(row == lane, 6.0, jnp.where(jnp.abs(row - lane) == 1, -1.0, 0.0)).astype(BF16)
    along_x = jnp.where((jnp.abs(row - lane) == 1) & (row // XS == lane // XS), -1.0, 0.0).astype(BF16)
    block = (PROBES, XS, YS)

    def around(z):
        if z == 0:
            return whole_rows(wide, 1)
        if z == DEPTH - 1:
            return whole_rows(wide, z - 1)
        return whole_rows(wide, z - 1) + whole_rows(wide, z + 1)

    def around_t(z):
        if z == 0:
            return whole_rows(wide, DEPTH + 1)
        if z == DEPTH - 1:
            return whole_rows(wide, DEPTH + z - 1)
        return whole_rows(wide, DEPTH + z - 1) + whole_rows(wide, DEPTH + z + 1)

    for z in range(DEPTH):
        w, t = whole_rows(wide, z), whole_rows(wide, DEPTH + z)
        both = jnp.concatenate([w.astype(BF16), t.astype(BF16)], axis=0)
        lap = jnp.dot(both, along_y, preferred_element_type=F32)
        lap = lap + jnp.dot(along_x, both, preferred_element_type=F32)
        w_lap = (lap[:BLOCK] - around(z)).reshape(block)
        t_lap = (lap[BLOCK:] - around_t(z)).reshape(block)
        w3, t3 = w.reshape(block), t.reshape(block)
        rise = t3 if z == 0 else t3 - whole_rows(wide, DEPTH + z - 1).reshape(block)
        image[z] = (visc[z][None] * w_lap + brink[z][None] * w3 - t3).reshape(BLOCK, YS)
        image[DEPTH + z] = (cond[z][None] * t_lap + 0.5 * w3 + flow[z][None] * rise).reshape(BLOCK, YS)


def inner(wide, flow, visc, brink, cond):
    whole = pl.BlockSpec(memory_space=pltpu.VMEM)
    return pl.pallas_call(
        inner_kernel,
        out_shape=pltpu.VMEM((SLABS, BLOCK, YS), F32),
        in_specs=[whole] * 5,
        out_specs=whole,
        compiler_params=params(),
        cost_estimate=pl.CostEstimate(flops=800_000_000, bytes_accessed=6_000_000, transcendentals=0),
        name="inner",
    )(wide, flow, visc, brink, cond)


def fold_lanes(half):
    lane = iota((8, BLOCK), 1)
    for step in (1, 2):
        ahead = pltpu.roll(half, BLOCK - step, 1)
        behind = pltpu.roll(half, step, 1)
        half = half + jnp.where(lane & step == 0, ahead, behind)
    return half


def gram_kernel(image, visc, cond, x_second, x_first, y_second, y_first, parts, gram, total):
    x_end, y_end = first_ends(parities())
    row, lane = iota((BLOCK, 2 * PROBES), 0), iota((BLOCK, 2 * PROBES), 1)
    target = jnp.where(lane < PROBES, x_end, XS - 1 - x_end)
    place = jnp.where((row % XS == target) & (row // XS == lane % PROBES), 1.0, 0.0).astype(BF16)
    columns = jnp.concatenate([y_first[...].astype(F32), y_second[...].astype(F32)], axis=0).T
    place = jnp.concatenate([place, columns.astype(BF16)], axis=1)
    row, lane = iota((64, YS), 0), iota((64, YS), 1)
    at_end = jnp.where(row < 32, y_end, YS - 1 - y_end) == lane
    for slab in range(SLABS):
        factor = visc[slab] if slab < DEPTH else cond[slab - DEPTH]
        span = pl.ds(slab * PROBES, PROBES)
        ends = jnp.where(at_end & (row % 32 == slab), 1.0, 0.0).astype(BF16)
        edges = jnp.concatenate([x_first[span, :], x_second[span, :], ends], axis=0)
        halo = jnp.dot(place, edges, preferred_element_type=F32).reshape(PROBES, XS, YS)
        full = image[slab] - (factor[None] * halo).reshape(BLOCK, YS)
        high = full.astype(BF16)
        parts[slab, :BLOCK] = high
        parts[slab, BLOCK:] = (full - high.astype(F32)).astype(BF16)
    for slab in range(SLABS):
        product = lax.dot_general(parts[slab], parts[slab, :BLOCK], NT, preferred_element_type=F32)
        if slab == 0:
            total[...] = product
        else:
            total[...] += product
    mixed = total[BLOCK:]
    square = total[:BLOCK] + mixed + mixed.T
    row, lane = iota((BLOCK, BLOCK), 0), iota((BLOCK, BLOCK), 1)
    square = jnp.where(row % XS == lane % XS, square, 0.0)
    square = jnp.sum(square.reshape(PROBES, XS, BLOCK), axis=1)
    top, bottom = square[:8], square[8:]
    first = iota((8, BLOCK), 1) % XS < XS // 2
    top = top + pltpu.roll(top, BLOCK - XS // 2, 1)
    bottom = bottom + pltpu.roll(bottom, XS // 2, 1)
    half = fold_lanes(jnp.where(first, top, bottom))
    half = jnp.where(iota((8, BLOCK), 1) % 4 == iota((8, BLOCK), 0) % 4, half, 0.0)
    half = half + pltpu.roll(half, 7, 0)
    half = half + pltpu.roll(half, 6, 0)
    gram[:, :BLOCK] = half[:1]
    gram[:, BLOCK:] = half[4:5]


def gram(image, visc, cond, halos):
    whole = pl.BlockSpec(memory_space=pltpu.VMEM)
    return pl.pallas_call(
        gram_kernel,
        out_shape=[
            pltpu.VMEM((SLABS, 2 * BLOCK, YS), BF16),
            jax.ShapeDtypeStruct((1, 2 * BLOCK), F32),
        ],
        in_specs=[whole] * 7,
        out_specs=[whole] * 2,
        scratch_shapes=[pltpu.VMEM((2 * BLOCK, BLOCK), F32)],
        compiler_params=params(),
        name="gram",
    )(image, visc, cond, *halos)


CHUNK = 4


def basis_kernel(scale, parts, pieces, basis, factor, result, small, sems):
    shape = (PROBES, BLOCK)
    row, lane = iota(shape, 0), iota(shape, 1)
    both = jnp.sum(pieces[...], axis=0)
    lane8, row8 = iota((8, BLOCK), 1), iota((8, BLOCK), 0)
    half = jnp.where(
        row8 < 4, jnp.broadcast_to(both[:, :BLOCK], (8, BLOCK)), jnp.broadcast_to(both[:, BLOCK:], (8, BLOCK))
    )
    half = fold_lanes(jnp.where(lane8 % 4 == row8 % 4, half, 0.0))
    first = lane8 % XS < XS // 2
    top = jnp.where(first, half, pltpu.roll(half, XS // 2, 1))
    bottom = jnp.where(first, pltpu.roll(half, BLOCK - XS // 2, 1), half)
    left = jnp.concatenate([top, bottom], axis=0)
    right = jnp.where(lane // XS == row, 1.0, 0.0).astype(F32)
    heads, crosses, tails = (jnp.ones(shape, F32) for _ in range(3))
    columns = [jnp.broadcast_to(left[:, k * XS : k * XS + 1], shape) for k in range(PROBES)]
    for k in range(0, PROBES, 2):
        one, two = columns[k : k + 2]
        head = jnp.broadcast_to(one[k : k + 1], shape)
        cross = jnp.broadcast_to(one[k + 1 : k + 2], shape)
        tail = jnp.broadcast_to(two[k + 1 : k + 2], shape)
        mine = row // 2 == k // 2
        heads = jnp.where(mine, head, heads)
        crosses = jnp.where(mine, cross, crosses)
        tails = jnp.where(mine, tail, tails)
        if k + 2 < PROBES:
            over = jnp.where(row > k + 1, 1.0 / (head * tail - cross * cross), 0.0)
            first_ratio = (tail * one - cross * two) * over
            second_ratio = (head * two - cross * one) * over
            for j in range(k + 2, PROBES):
                columns[j] = (
                    columns[j]
                    - first_ratio * jnp.broadcast_to(one[j : j + 1], shape)
                    - second_ratio * jnp.broadcast_to(two[j : j + 1], shape)
                )
            left, right = (
                side
                - first_ratio * jnp.broadcast_to(side[k : k + 1], shape)
                - second_ratio * jnp.broadcast_to(side[k + 1 : k + 2], shape)
                for side in (left, right)
            )
    odd = row % 2 == 1
    ratio = jnp.where(odd, crosses / heads, 0.0)
    left, right = (side - ratio * pltpu.roll(side, 1, 0) for side in (left, right))
    pivots = jnp.where(odd, tails - ratio * crosses, heads)
    root = lax.rsqrt(pivots)
    root = root * (1.5 - 0.5 * pivots * root * root)
    right = right * (root * scale)
    mask = jnp.where(iota((XS, BLOCK), 1) % XS == iota((XS, BLOCK), 0), 1.0, 0.0)
    weight = jnp.concatenate([mask * right[q : q + 1] for q in range(PROBES)], axis=0)
    high = weight.astype(BF16)
    low = (weight - high.astype(F32)).astype(BF16)
    weight = jnp.concatenate(
        [jnp.concatenate([high, high], axis=1), jnp.concatenate([low, low], axis=1)], axis=0
    )

    copies = []
    for slab in range(SLABS):
        out = jnp.dot(weight, parts[slab], preferred_element_type=F32)
        out = out[:BLOCK] + out[BLOCK:]
        result[:, slab] = out.reshape(PROBES, XS, YS)
        if slab % CHUNK == CHUNK - 1:
            span = pl.ds(slab - CHUNK + 1, CHUNK)
            copy = pltpu.make_async_copy(result.at[:, span], basis.at[:, span], sems.at[slab // CHUNK])
            copy.start()
            copies.append(copy)
        if slab == CHUNK:
            upper = jnp.where(lane // XS >= row, left * (root * (1.0 / scale)), 0.0)
            chosen = jnp.where(iota((BLOCK, PROBES), 0) == XS * iota((BLOCK, PROBES), 1), 1.0, 0.0)
            small[...] = jnp.dot(upper, chosen, precision=lax.Precision.HIGHEST, preferred_element_type=F32)
            copy = pltpu.make_async_copy(small, factor, sems.at[SLABS // CHUNK])
            copy.start()
            copies.append(copy)
    for copy in copies:
        copy.wait()


def orthonormal(parts, pieces, scale):
    whole = pl.BlockSpec(memory_space=pltpu.VMEM)
    return pl.pallas_call(
        functools.partial(basis_kernel, scale),
        out_shape=[
            jax.ShapeDtypeStruct((PROBES, SLABS, XS, YS), F32),
            jax.ShapeDtypeStruct((PROBES, PROBES), F32),
        ],
        in_specs=[whole, whole],
        out_specs=[pl.BlockSpec(memory_space=pl.ANY)] * 2,
        scratch_shapes=[
            pltpu.VMEM((PROBES, SLABS, XS, YS), F32),
            pltpu.VMEM((PROBES, PROBES), F32),
            pltpu.SemaphoreType.DMA((SLABS // CHUNK + 1,)),
        ],
        compiler_params=params(),
        name="orthonormal",
    )(parts, pieces)


def swap(array, axis, first):
    count = lax.axis_size(axis)
    pairs = [(i, i + 1) for i in range(0 if first else 1, count - 1, 2)]
    return lax.ppermute(array, axis, pairs + [(j, i) for i, j in pairs])


def all_copies(array, axes):
    copies = jnp.broadcast_to(array[None], (lax.axis_size(axes),) + array.shape)
    return lax.all_to_all(copies, axes, 0, 0)


def on_device(probes, material, visc_table, brink_table, cond_table, base_flow):
    shape = probes.shape
    probes = probes.reshape(PROBES, SLABS, XS, YS)
    x_second, wide, flow, kind, tables = load(probes, material, base_flow, (visc_table, brink_table, cond_table))
    x_second = swap(x_second, GX, False)
    x_first, y_first, y_second, visc, brink, cond = faces(wide, kind, tables)
    x_first = swap(x_first, GX, True)
    y_second = swap(y_second, GY, False)
    y_first = swap(y_first, GY, True)
    halos = (x_second, x_first, y_second, y_first)
    image = inner(wide, flow, visc, brink, cond)
    parts, local = gram(image, visc, cond, halos)
    slab_sum = jnp.sum(all_copies(local, ("y", "core")), axis=0)
    pieces = all_copies(slab_sum, ("x", "z"))
    rows_total = SLABS * XS * YS * lax.axis_size(GX) * lax.axis_size(GY)
    basis, factor = orthonormal(parts, pieces, math.sqrt(rows_total))
    return (basis.reshape(shape), factor)


def solution(mesh):
    rows, columns = mesh.shape["gx"], mesh.shape["gy"]
    wide, cores = (4 if rows % 4 == 0 else 1), (2 if columns % 2 == 0 else 1)
    mesh = jax.sharding.Mesh(
        mesh.devices.reshape(rows // wide, wide, columns // cores, cores), ("y", "x", "z", "core")
    )
    grid = P(None, GX, GY)
    in_specs = (P(None, None, None, GX, GY), grid, P(), P(), P(), grid)
    out_specs = (P(None, None, None, GX, GY), P())
    return jax.shard_map(
        on_device, mesh=mesh, in_specs=in_specs, out_specs=out_specs, check_vma=False
    )
```

```python
import functools
import math

import jax
import jax.numpy as jnp
from jax import lax
from jax.experimental import pallas as pl
from jax.experimental.pallas import tpu as pltpu
from jax.sharding import PartitionSpec as P

GX = ("y", "x")
GY = ("z", "core")
PROBES = 16
SLABS = 24
DEPTH = 12
XS = 8
YS = 256
BLOCK = PROBES * XS
F32 = jnp.float32
BF16 = jnp.bfloat16
NT = (((1,), (1,)), ((), ()))


def iota(shape, dim):
    return lax.broadcasted_iota(jnp.int32, shape, dim)


def params():
    return pltpu.CompilerParams(vmem_limit_bytes=24 * 1024 * 1024)


def pick(material, table):
    value = jnp.where(material == 0, table[0], table[1])
    value = jnp.where(material == 2, table[2], value)
    return jnp.where(material == 3, table[3], value)


def first_ends(parity):
    return (XS - 1) * (1 - parity[0]), (YS - 1) * (1 - parity[1])


def parities():
    return lax.axis_index(GX) % 2, lax.axis_index(GY) % 2


LOADS = 4


def whole_rows(wide, slab):
    return jnp.concatenate([wide[0, slab], wide[1, slab]], axis=1)


def load_kernel(
    probes, material, flow_in, visc_in, brink_in, cond_in,
    x_first, x_second, y_first, y_second, wide, flow, visc, brink, cond, along_y, along_x, ends_at,
    kind, tables, packed, columns, sems,
):
    each = PROBES // LOADS
    loads = [
        pltpu.make_async_copy(probes.at[pl.ds(i * each, each)], packed.at[pl.ds(i * each, each)], sems.at[i])
        for i in range(LOADS)
    ]
    others = ((material, kind), (visc_in, tables.at[0]), (brink_in, tables.at[1]), (cond_in, tables.at[2]), (flow_in, flow))
    others = [pltpu.make_async_copy(src, dst, sems.at[LOADS + i]) for i, (src, dst) in enumerate(others)]
    for copy in loads + others:
        copy.start()
    x_end, y_end = first_ends(parities())
    row, lane = iota((YS, YS), 0), iota((YS, YS), 1)
    along_y[...] = jnp.where(row == lane, 6.0, jnp.where(jnp.abs(row - lane) == 1, -1.0, 0.0)).astype(BF16)
    along_x[...] = jnp.where((jnp.abs(row - lane) == 1) & (row // XS == lane // XS), -1.0, 0.0).astype(BF16)
    row, lane = iota((64, YS), 0), iota((64, YS), 1)
    at_end = jnp.where(row < 32, y_end, YS - 1 - y_end) == lane
    for slab in range(SLABS):
        ends_at[slab] = jnp.where(at_end & (row % 32 == slab), 1.0, 0.0).astype(BF16)
    lane = iota((XS, 128), 1)
    for i, copy in enumerate(loads):
        copy.wait()
        for probe in range(i * each, (i + 1) * each):
            field = packed[probe].astype(F32)
            rows = slice(probe * XS, (probe + 1) * XS)
            wide[0, :, rows, :] = field[:, :, :128]
            wide[1, :, rows, :] = field[:, :, 128:]
            ends = jnp.where(lane < 64, field[:, :, :128], field[:, :, 128:])
            sides = jnp.zeros((XS, 128), F32)
            for slab in range(SLABS):
                sides = jnp.where(lane // 2 == slab, pltpu.roll(ends[slab], 2 * slab + 1, 1), sides)
            columns[rows] = sides
    x_face(wide, XS - 1 - x_end, x_second)
    x_face(wide, x_end, x_first)
    columns[...] = columns[...].T
    high, low = columns[pl.ds(0, 32, stride=2), :], columns[pl.ds(1, 32, stride=2), :]
    y_first[...] = jnp.where(y_end == 0, low, high).astype(BF16)
    y_second[...] = jnp.where(y_end == 0, high, low).astype(BF16)
    for copy in others:
        copy.wait()
    for i, value in enumerate((visc, brink, cond)):
        value[...] = pick(kind[...], [tables[i, j] for j in range(4)])


def x_face(wide, end, face):
    rows = wide.reshape(2, SLABS * BLOCK, 128)
    for half in range(2):
        ends = rows[half, pl.ds(end, SLABS * PROBES, stride=XS), :]
        face[:, half * 128 : half * 128 + 128] = ends.astype(BF16)


def load(probes, material, flow, tables):
    cells = (DEPTH, XS, YS)
    arrays = [pltpu.with_memory_space_constraint(a, pltpu.HBM) for a in (probes, material, flow, *tables)]
    whole = pl.BlockSpec(memory_space=pltpu.VMEM)
    return pl.pallas_call(
        load_kernel,
        out_shape=[pltpu.VMEM((SLABS * PROBES, YS), BF16)] * 2
        + [pltpu.VMEM((32, BLOCK), BF16)] * 2
        + [pltpu.VMEM((2, SLABS, BLOCK, 128), F32)]
        + [pltpu.VMEM(cells, F32)] * 4
        + [pltpu.VMEM((YS, YS), BF16)] * 2
        + [pltpu.VMEM((SLABS, 64, YS), BF16)],
        in_specs=[pl.BlockSpec(memory_space=pl.ANY)] * 6,
        out_specs=[whole] * 12,
        scratch_shapes=[
            pltpu.VMEM(cells, jnp.int32),
            pltpu.SMEM((3, 4), F32),
            pltpu.VMEM((PROBES, SLABS, XS, YS), BF16),
            pltpu.VMEM((BLOCK, 128), F32),
            pltpu.SemaphoreType.DMA((LOADS + 5,)),
        ],
        compiler_params=params(),
        name="load",
    )(*arrays)


def inner_kernel(wide, flow, visc, brink, cond, along_y, along_x, image):
    block = (PROBES, XS, YS)

    def around(z):
        if z == 0:
            return whole_rows(wide, 1)
        if z == DEPTH - 1:
            return whole_rows(wide, z - 1)
        return whole_rows(wide, z - 1) + whole_rows(wide, z + 1)

    def around_t(z):
        if z == 0:
            return whole_rows(wide, DEPTH + 1)
        if z == DEPTH - 1:
            return whole_rows(wide, DEPTH + z - 1)
        return whole_rows(wide, DEPTH + z - 1) + whole_rows(wide, DEPTH + z + 1)

    for z in range(DEPTH):
        w, t = whole_rows(wide, z), whole_rows(wide, DEPTH + z)
        both = jnp.concatenate([w.astype(BF16), t.astype(BF16)], axis=0)
        lap = jnp.dot(both, along_y[...], preferred_element_type=F32)
        lap = lap + jnp.dot(along_x[...], both, preferred_element_type=F32)
        w_lap = (lap[:BLOCK] - around(z)).reshape(block)
        t_lap = (lap[BLOCK:] - around_t(z)).reshape(block)
        w3, t3 = w.reshape(block), t.reshape(block)
        rise = t3 if z == 0 else t3 - whole_rows(wide, DEPTH + z - 1).reshape(block)
        image[z] = (visc[z][None] * w_lap + brink[z][None] * w3 - t3).reshape(BLOCK, YS)
        image[DEPTH + z] = (cond[z][None] * t_lap + 0.5 * w3 + flow[z][None] * rise).reshape(BLOCK, YS)


def inner(*arrays):
    whole = pl.BlockSpec(memory_space=pltpu.VMEM)
    return pl.pallas_call(
        inner_kernel,
        out_shape=pltpu.VMEM((SLABS, BLOCK, YS), F32),
        in_specs=[whole] * 7,
        out_specs=whole,
        compiler_params=params(),
        cost_estimate=pl.CostEstimate(flops=800_000_000, bytes_accessed=6_000_000, transcendentals=0),
        name="inner",
    )(*arrays)


def fold_lanes(half):
    lane = iota((8, BLOCK), 1)
    for step in (1, 2):
        ahead = pltpu.roll(half, BLOCK - step, 1)
        behind = pltpu.roll(half, step, 1)
        half = half + jnp.where(lane & step == 0, ahead, behind)
    return half


def gram_kernel(image, visc, cond, ends_at, x_second, x_first, y_second, y_first, parts, gram, total):
    x_end, _ = first_ends(parities())
    row, lane = iota((BLOCK, 2 * PROBES), 0), iota((BLOCK, 2 * PROBES), 1)
    target = jnp.where(lane < PROBES, x_end, XS - 1 - x_end)
    place = jnp.where((row % XS == target) & (row // XS == lane % PROBES), 1.0, 0.0).astype(BF16)
    columns = jnp.concatenate([y_first[...].astype(F32), y_second[...].astype(F32)], axis=0).T
    place = jnp.concatenate([place, columns.astype(BF16)], axis=1)
    for slab in range(SLABS):
        factor = visc[slab] if slab < DEPTH else cond[slab - DEPTH]
        span = pl.ds(slab * PROBES, PROBES)
        edges = jnp.concatenate([x_first[span, :], x_second[span, :], ends_at[slab]], axis=0)
        halo = jnp.dot(place, edges, preferred_element_type=F32).reshape(PROBES, XS, YS)
        full = image[slab] - (factor[None] * halo).reshape(BLOCK, YS)
        high = full.astype(BF16)
        parts[slab, :BLOCK] = high
        parts[slab, BLOCK:] = (full - high.astype(F32)).astype(BF16)
    for slab in range(SLABS):
        product = lax.dot_general(parts[slab], parts[slab, :BLOCK], NT, preferred_element_type=F32)
        if slab == 0:
            total[...] = product
        else:
            total[...] += product
    mixed = total[BLOCK:]
    square = total[:BLOCK] + mixed + mixed.T
    row, lane = iota((BLOCK, BLOCK), 0), iota((BLOCK, BLOCK), 1)
    square = jnp.where(row % XS == lane % XS, square, 0.0)
    square = jnp.sum(square.reshape(PROBES, XS, BLOCK), axis=1)
    top, bottom = square[:8], square[8:]
    first = iota((8, BLOCK), 1) % XS < XS // 2
    top = top + pltpu.roll(top, BLOCK - XS // 2, 1)
    bottom = bottom + pltpu.roll(bottom, XS // 2, 1)
    half = fold_lanes(jnp.where(first, top, bottom))
    half = jnp.where(iota((8, BLOCK), 1) % 4 == iota((8, BLOCK), 0) % 4, half, 0.0)
    half = half + pltpu.roll(half, 7, 0)
    half = half + pltpu.roll(half, 6, 0)
    gram[:, :BLOCK] = half[:1]
    gram[:, BLOCK:] = half[4:5]


def gram(image, visc, cond, ends_at, halos):
    whole = pl.BlockSpec(memory_space=pltpu.VMEM)
    return pl.pallas_call(
        gram_kernel,
        out_shape=[
            pltpu.VMEM((SLABS, 2 * BLOCK, YS), BF16),
            jax.ShapeDtypeStruct((1, 2 * BLOCK), F32),
        ],
        in_specs=[whole] * 8,
        out_specs=[whole] * 2,
        scratch_shapes=[pltpu.VMEM((2 * BLOCK, BLOCK), F32)],
        compiler_params=params(),
        name="gram",
    )(image, visc, cond, ends_at, *halos)


CHUNK = 4


def basis_kernel(scale, parts, pieces, basis, factor, result, small, sems):
    shape = (PROBES, BLOCK)
    row, lane = iota(shape, 0), iota(shape, 1)
    both = jnp.sum(pieces[...], axis=0)
    lane8, row8 = iota((8, BLOCK), 1), iota((8, BLOCK), 0)
    half = jnp.where(
        row8 < 4, jnp.broadcast_to(both[:, :BLOCK], (8, BLOCK)), jnp.broadcast_to(both[:, BLOCK:], (8, BLOCK))
    )
    half = fold_lanes(jnp.where(lane8 % 4 == row8 % 4, half, 0.0))
    first = lane8 % XS < XS // 2
    top = jnp.where(first, half, pltpu.roll(half, XS // 2, 1))
    bottom = jnp.where(first, pltpu.roll(half, BLOCK - XS // 2, 1), half)
    left = jnp.concatenate([top, bottom], axis=0)
    right = jnp.where(lane // XS == row, 1.0, 0.0).astype(F32)
    heads, crosses, tails = (jnp.ones(shape, F32) for _ in range(3))
    columns = [jnp.broadcast_to(left[:, k * XS : k * XS + 1], shape) for k in range(PROBES)]
    for k in range(0, PROBES, 2):
        one, two = columns[k : k + 2]
        head = jnp.broadcast_to(one[k : k + 1], shape)
        cross = jnp.broadcast_to(one[k + 1 : k + 2], shape)
        tail = jnp.broadcast_to(two[k + 1 : k + 2], shape)
        mine = row // 2 == k // 2
        heads = jnp.where(mine, head, heads)
        crosses = jnp.where(mine, cross, crosses)
        tails = jnp.where(mine, tail, tails)
        if k + 2 < PROBES:
            over = jnp.where(row > k + 1, 1.0 / (head * tail - cross * cross), 0.0)
            first_ratio = (tail * one - cross * two) * over
            second_ratio = (head * two - cross * one) * over
            for j in range(k + 2, PROBES):
                columns[j] = (
                    columns[j]
                    - first_ratio * jnp.broadcast_to(one[j : j + 1], shape)
                    - second_ratio * jnp.broadcast_to(two[j : j + 1], shape)
                )
            left, right = (
                side
                - first_ratio * jnp.broadcast_to(side[k : k + 1], shape)
                - second_ratio * jnp.broadcast_to(side[k + 1 : k + 2], shape)
                for side in (left, right)
            )
    odd = row % 2 == 1
    ratio = jnp.where(odd, crosses / heads, 0.0)
    left, right = (side - ratio * pltpu.roll(side, 1, 0) for side in (left, right))
    pivots = jnp.where(odd, tails - ratio * crosses, heads)
    root = lax.rsqrt(pivots)
    root = root * (1.5 - 0.5 * pivots * root * root)
    right = right * (root * scale)
    mask = jnp.where(iota((XS, BLOCK), 1) % XS == iota((XS, BLOCK), 0), 1.0, 0.0)
    weight = jnp.concatenate([mask * right[q : q + 1] for q in range(PROBES)], axis=0)
    high = weight.astype(BF16)
    low = (weight - high.astype(F32)).astype(BF16)
    weight = jnp.concatenate(
        [jnp.concatenate([high, high], axis=1), jnp.concatenate([low, low], axis=1)], axis=0
    )

    copies = []
    for slab in range(SLABS):
        out = jnp.dot(weight, parts[slab], preferred_element_type=F32)
        out = out[:BLOCK] + out[BLOCK:]
        result[:, slab] = out.reshape(PROBES, XS, YS)
        if slab % CHUNK == CHUNK - 1:
            span = pl.ds(slab - CHUNK + 1, CHUNK)
            copy = pltpu.make_async_copy(result.at[:, span], basis.at[:, span], sems.at[slab // CHUNK])
            copy.start()
            copies.append(copy)
        if slab == CHUNK:
            upper = jnp.where(lane // XS >= row, left * (root * (1.0 / scale)), 0.0)
            chosen = jnp.where(iota((BLOCK, PROBES), 0) == XS * iota((BLOCK, PROBES), 1), 1.0, 0.0)
            small[...] = jnp.dot(upper, chosen, precision=lax.Precision.HIGHEST, preferred_element_type=F32)
            copy = pltpu.make_async_copy(small, factor, sems.at[SLABS // CHUNK])
            copy.start()
            copies.append(copy)
    for copy in copies:
        copy.wait()


def orthonormal(parts, pieces, scale):
    whole = pl.BlockSpec(memory_space=pltpu.VMEM)
    return pl.pallas_call(
        functools.partial(basis_kernel, scale),
        out_shape=[
            jax.ShapeDtypeStruct((PROBES, SLABS, XS, YS), F32),
            jax.ShapeDtypeStruct((PROBES, PROBES), F32),
        ],
        in_specs=[whole, whole],
        out_specs=[pl.BlockSpec(memory_space=pl.ANY)] * 2,
        scratch_shapes=[
            pltpu.VMEM((PROBES, SLABS, XS, YS), F32),
            pltpu.VMEM((PROBES, PROBES), F32),
            pltpu.SemaphoreType.DMA((SLABS // CHUNK + 1,)),
        ],
        compiler_params=params(),
        name="orthonormal",
    )(parts, pieces)


def swap(array, axis, first):
    count = lax.axis_size(axis)
    pairs = [(i, i + 1) for i in range(0 if first else 1, count - 1, 2)]
    return lax.ppermute(array, axis, pairs + [(j, i) for i, j in pairs])


def all_copies(array, axes):
    copies = jnp.broadcast_to(array[None], (lax.axis_size(axes),) + array.shape)
    return lax.all_to_all(copies, axes, 0, 0)


def on_device(probes, material, visc_table, brink_table, cond_table, base_flow):
    shape = probes.shape
    probes = probes.reshape(PROBES, SLABS, XS, YS)
    x_first, x_second, y_first, y_second, wide, flow, visc, brink, cond, along_y, along_x, ends_at = load(
        probes, material, base_flow, (visc_table, brink_table, cond_table)
    )
    x_second = swap(x_second, GX, False)
    x_first = swap(x_first, GX, True)
    y_second = swap(y_second, GY, False)
    y_first = swap(y_first, GY, True)
    halos = (x_second, x_first, y_second, y_first)
    image = inner(wide, flow, visc, brink, cond, along_y, along_x)
    parts, local = gram(image, visc, cond, ends_at, halos)
    slab_sum = jnp.sum(all_copies(local, ("core", "y")), axis=0)
    pieces = all_copies(slab_sum, ("z", "x"))
    rows_total = SLABS * XS * YS * lax.axis_size(GX) * lax.axis_size(GY)
    basis, factor = orthonormal(parts, pieces, math.sqrt(rows_total))
    return (basis.reshape(shape), factor)


def solution(mesh):
    rows, columns = mesh.shape["gx"], mesh.shape["gy"]
    wide, cores = (4 if rows % 4 == 0 else 1), (2 if columns % 2 == 0 else 1)
    mesh = jax.sharding.Mesh(
        mesh.devices.reshape(rows // wide, wide, columns // cores, cores), ("y", "x", "z", "core")
    )
    grid = P(None, GX, GY)
    in_specs = (P(None, None, None, GX, GY), grid, P(), P(), P(), grid)
    out_specs = (P(None, None, None, GX, GY), P())
    return jax.shard_map(
        on_device, mesh=mesh, in_specs=in_specs, out_specs=out_specs, check_vma=False
    )
```

```python
import functools
import math

import jax
import jax.numpy as jnp
from jax import lax
from jax.experimental import pallas as pl
from jax.experimental.pallas import tpu as pltpu
from jax.sharding import PartitionSpec as P

GX = ("y", "x")
GY = ("z", "core")
PROBES = 16
SLABS = 24
DEPTH = 12
XS = 8
YS = 256
BLOCK = PROBES * XS
F32 = jnp.float32
BF16 = jnp.bfloat16
NT = (((1,), (1,)), ((), ()))


def iota(shape, dim):
    return lax.broadcasted_iota(jnp.int32, shape, dim)


def params():
    return pltpu.CompilerParams(vmem_limit_bytes=24 * 1024 * 1024)


def pick(material, table):
    value = jnp.where(material == 0, table[0], table[1])
    value = jnp.where(material == 2, table[2], value)
    return jnp.where(material == 3, table[3], value)


def first_ends(parity):
    return (XS - 1) * (1 - parity[0]), (YS - 1) * (1 - parity[1])


def parities():
    return lax.axis_index(GX) % 2, lax.axis_index(GY) % 2


LOADS = 4


def whole_rows(wide, slab):
    return jnp.concatenate([wide[0, slab], wide[1, slab]], axis=1)


def load_kernel(
    probes, material, flow_in, visc_in, brink_in, cond_in,
    x_first, x_second, y_first, y_second, wide, flow, visc, brink, cond, along_y, along_x, ends_at,
    kind, tables, packed, columns, sems,
):
    each = PROBES // LOADS
    loads = [
        pltpu.make_async_copy(probes.at[pl.ds(i * each, each)], packed.at[pl.ds(i * each, each)], sems.at[i])
        for i in range(LOADS)
    ]
    others = ((material, kind), (visc_in, tables.at[0]), (brink_in, tables.at[1]), (cond_in, tables.at[2]), (flow_in, flow))
    others = [pltpu.make_async_copy(src, dst, sems.at[LOADS + i]) for i, (src, dst) in enumerate(others)]
    for copy in loads + others:
        copy.start()
    x_end, y_end = first_ends(parities())
    row, lane = iota((YS, YS), 0), iota((YS, YS), 1)
    along_y[...] = jnp.where(row == lane, 6.0, jnp.where(jnp.abs(row - lane) == 1, -1.0, 0.0)).astype(BF16)
    along_x[...] = jnp.where((jnp.abs(row - lane) == 1) & (row // XS == lane // XS), -1.0, 0.0).astype(BF16)
    row, lane = iota((64, YS), 0), iota((64, YS), 1)
    at_end = jnp.where(row < 32, y_end, YS - 1 - y_end) == lane
    for slab in range(SLABS):
        ends_at[slab] = jnp.where(at_end & (row % 32 == slab), 1.0, 0.0).astype(BF16)
    lane = iota((XS, 128), 1)
    for i, copy in enumerate(loads):
        copy.wait()
        for probe in range(i * each, (i + 1) * each):
            field = packed[probe].astype(F32)
            rows = slice(probe * XS, (probe + 1) * XS)
            wide[0, :, rows, :] = field[:, :, :128]
            wide[1, :, rows, :] = field[:, :, 128:]
            ends = jnp.where(lane < 64, field[:, :, :128], field[:, :, 128:])
            sides = jnp.zeros((XS, 128), F32)
            for slab in range(SLABS):
                sides = jnp.where(lane // 2 == slab, pltpu.roll(ends[slab], 2 * slab + 1, 1), sides)
            columns[rows] = sides
    x_face(wide, XS - 1 - x_end, x_second)
    x_face(wide, x_end, x_first)
    columns[...] = columns[...].T
    high, low = columns[pl.ds(0, 32, stride=2), :], columns[pl.ds(1, 32, stride=2), :]
    y_first[...] = jnp.where(y_end == 0, low, high).astype(BF16)
    y_second[...] = jnp.where(y_end == 0, high, low).astype(BF16)
    for copy in others:
        copy.wait()
    for i, value in enumerate((visc, brink, cond)):
        value[...] = pick(kind[...], [tables[i, j] for j in range(4)])


def x_face(wide, end, face):
    rows = wide.reshape(2, SLABS * BLOCK, 128)
    for half in range(2):
        ends = rows[half, pl.ds(end, SLABS * PROBES, stride=XS), :]
        face[:, half * 128 : half * 128 + 128] = ends.astype(BF16)


def load(probes, material, flow, tables):
    cells = (DEPTH, XS, YS)
    arrays = [pltpu.with_memory_space_constraint(a, pltpu.HBM) for a in (probes, material, flow, *tables)]
    whole = pl.BlockSpec(memory_space=pltpu.VMEM)
    return pl.pallas_call(
        load_kernel,
        out_shape=[pltpu.VMEM((SLABS * PROBES, YS), BF16)] * 2
        + [pltpu.VMEM((32, BLOCK), BF16)] * 2
        + [pltpu.VMEM((2, SLABS, BLOCK, 128), F32)]
        + [pltpu.VMEM(cells, F32)] * 4
        + [pltpu.VMEM((YS, YS), BF16)] * 2
        + [pltpu.VMEM((SLABS, 64, YS), BF16)],
        in_specs=[pl.BlockSpec(memory_space=pl.ANY)] * 6,
        out_specs=[whole] * 12,
        scratch_shapes=[
            pltpu.VMEM(cells, jnp.int32),
            pltpu.SMEM((3, 4), F32),
            pltpu.VMEM((PROBES, SLABS, XS, YS), BF16),
            pltpu.VMEM((BLOCK, 128), F32),
            pltpu.SemaphoreType.DMA((LOADS + 5,)),
        ],
        compiler_params=params(),
        name="load",
    )(*arrays)


def inner_kernel(wide, flow, visc, brink, cond, along_y, along_x, image):
    block = (PROBES, XS, YS)

    def around(z):
        if z == 0:
            return whole_rows(wide, 1)
        if z == DEPTH - 1:
            return whole_rows(wide, z - 1)
        return whole_rows(wide, z - 1) + whole_rows(wide, z + 1)

    def around_t(z):
        if z == 0:
            return whole_rows(wide, DEPTH + 1)
        if z == DEPTH - 1:
            return whole_rows(wide, DEPTH + z - 1)
        return whole_rows(wide, DEPTH + z - 1) + whole_rows(wide, DEPTH + z + 1)

    for z in range(DEPTH):
        w, t = whole_rows(wide, z), whole_rows(wide, DEPTH + z)
        both = jnp.concatenate([w.astype(BF16), t.astype(BF16)], axis=0)
        lap = jnp.dot(both, along_y[...], preferred_element_type=F32)
        lap = lap + jnp.dot(along_x[...], both, preferred_element_type=F32)
        w_lap = (lap[:BLOCK] - around(z)).reshape(block)
        t_lap = (lap[BLOCK:] - around_t(z)).reshape(block)
        w3, t3 = w.reshape(block), t.reshape(block)
        rise = t3 if z == 0 else t3 - whole_rows(wide, DEPTH + z - 1).reshape(block)
        image[z] = (visc[z][None] * w_lap + brink[z][None] * w3 - t3).reshape(BLOCK, YS)
        image[DEPTH + z] = (cond[z][None] * t_lap + 0.5 * w3 + flow[z][None] * rise).reshape(BLOCK, YS)


def inner(*arrays):
    whole = pl.BlockSpec(memory_space=pltpu.VMEM)
    return pl.pallas_call(
        inner_kernel,
        out_shape=pltpu.VMEM((SLABS, BLOCK, YS), F32),
        in_specs=[whole] * 7,
        out_specs=whole,
        compiler_params=params(),
        cost_estimate=pl.CostEstimate(flops=800_000_000, bytes_accessed=6_000_000, transcendentals=0),
        name="inner",
    )(*arrays)


def fold_lanes(half):
    lane = iota((8, BLOCK), 1)
    for step in (1, 2):
        ahead = pltpu.roll(half, BLOCK - step, 1)
        behind = pltpu.roll(half, step, 1)
        half = half + jnp.where(lane & step == 0, ahead, behind)
    return half


def gram_kernel(image, visc, cond, ends_at, x_second, x_first, y_second, y_first, parts, gram, total):
    x_end, _ = first_ends(parities())
    row, lane = iota((BLOCK, 2 * PROBES), 0), iota((BLOCK, 2 * PROBES), 1)
    target = jnp.where(lane < PROBES, x_end, XS - 1 - x_end)
    place = jnp.where((row % XS == target) & (row // XS == lane % PROBES), 1.0, 0.0).astype(BF16)
    columns = jnp.concatenate([y_first[...].astype(F32), y_second[...].astype(F32)], axis=0).T
    place = jnp.concatenate([place, columns.astype(BF16)], axis=1)
    for slab in range(SLABS):
        factor = visc[slab] if slab < DEPTH else cond[slab - DEPTH]
        span = pl.ds(slab * PROBES, PROBES)
        edges = jnp.concatenate([x_first[span, :], x_second[span, :], ends_at[slab]], axis=0)
        halo = jnp.dot(place, edges, preferred_element_type=F32).reshape(PROBES, XS, YS)
        full = image[slab] - (factor[None] * halo).reshape(BLOCK, YS)
        high = full.astype(BF16)
        parts[slab, :BLOCK] = high
        parts[slab, BLOCK:] = (full - high.astype(F32)).astype(BF16)
    for slab in range(SLABS):
        product = lax.dot_general(parts[slab], parts[slab, :BLOCK], NT, preferred_element_type=F32)
        if slab == 0:
            total[...] = product
        else:
            total[...] += product
    mixed = total[BLOCK:]
    square = total[:BLOCK] + mixed + mixed.T
    row, lane = iota((BLOCK, BLOCK), 0), iota((BLOCK, BLOCK), 1)
    square = jnp.where(row % XS == lane % XS, square, 0.0)
    square = jnp.sum(square.reshape(PROBES, XS, BLOCK), axis=1)
    top, bottom = square[:8], square[8:]
    first = iota((8, BLOCK), 1) % XS < XS // 2
    top = top + pltpu.roll(top, BLOCK - XS // 2, 1)
    bottom = bottom + pltpu.roll(bottom, XS // 2, 1)
    half = fold_lanes(jnp.where(first, top, bottom))
    half = jnp.where(iota((8, BLOCK), 1) % 4 == iota((8, BLOCK), 0) % 4, half, 0.0)
    half = half + pltpu.roll(half, 7, 0)
    half = half + pltpu.roll(half, 6, 0)
    gram[:, :BLOCK] = half[:1]
    gram[:, BLOCK:] = half[4:5]


def gram(image, visc, cond, ends_at, halos):
    whole = pl.BlockSpec(memory_space=pltpu.VMEM)
    return pl.pallas_call(
        gram_kernel,
        out_shape=[
            pltpu.VMEM((SLABS, 2 * BLOCK, YS), BF16),
            jax.ShapeDtypeStruct((1, 2 * BLOCK), F32),
        ],
        in_specs=[whole] * 8,
        out_specs=[whole] * 2,
        scratch_shapes=[pltpu.VMEM((2 * BLOCK, BLOCK), F32)],
        compiler_params=params(),
        name="gram",
    )(image, visc, cond, ends_at, *halos)


CHUNK = 4


def basis_kernel(scale, parts, pieces, basis, factor, result, small, sems):
    shape = (PROBES, BLOCK)
    row, lane = iota(shape, 0), iota(shape, 1)
    both = jnp.sum(pieces[...], axis=0)
    lane8, row8 = iota((8, BLOCK), 1), iota((8, BLOCK), 0)
    half = jnp.where(
        row8 < 4, jnp.broadcast_to(both[:, :BLOCK], (8, BLOCK)), jnp.broadcast_to(both[:, BLOCK:], (8, BLOCK))
    )
    half = fold_lanes(jnp.where(lane8 % 4 == row8 % 4, half, 0.0))
    first = lane8 % XS < XS // 2
    top = jnp.where(first, half, pltpu.roll(half, XS // 2, 1))
    bottom = jnp.where(first, pltpu.roll(half, BLOCK - XS // 2, 1), half)
    left = jnp.concatenate([top, bottom], axis=0)
    right = jnp.where(lane // XS == row, 1.0, 0.0).astype(F32)
    heads, crosses, tails = (jnp.ones(shape, F32) for _ in range(3))
    columns = [jnp.broadcast_to(left[:, k * XS : k * XS + 1], shape) for k in range(PROBES)]
    for k in range(0, PROBES, 2):
        one, two = columns[k : k + 2]
        head = jnp.broadcast_to(one[k : k + 1], shape)
        cross = jnp.broadcast_to(one[k + 1 : k + 2], shape)
        tail = jnp.broadcast_to(two[k + 1 : k + 2], shape)
        mine = row // 2 == k // 2
        heads = jnp.where(mine, head, heads)
        crosses = jnp.where(mine, cross, crosses)
        tails = jnp.where(mine, tail, tails)
        if k + 2 < PROBES:
            inverse = 1.0 / head
            lean = cross * inverse
            over = jnp.where(row > k + 1, 1.0 / (tail - lean * cross), 0.0)
            second_ratio = (two - lean * one) * over
            first_ratio = jnp.where(row > k + 1, one * inverse, 0.0) - lean * second_ratio
            for j in range(k + 2, PROBES):
                columns[j] = (
                    columns[j]
                    - first_ratio * jnp.broadcast_to(one[j : j + 1], shape)
                    - second_ratio * jnp.broadcast_to(two[j : j + 1], shape)
                )
            left, right = (
                side
                - first_ratio * jnp.broadcast_to(side[k : k + 1], shape)
                - second_ratio * jnp.broadcast_to(side[k + 1 : k + 2], shape)
                for side in (left, right)
            )
    odd = row % 2 == 1
    ratio = jnp.where(odd, crosses / heads, 0.0)
    left, right = (side - ratio * pltpu.roll(side, 1, 0) for side in (left, right))
    pivots = jnp.where(odd, tails - ratio * crosses, heads)
    root = lax.rsqrt(pivots)
    root = root * (1.5 - 0.5 * pivots * root * root)
    right = right * (root * scale)
    mask = jnp.where(iota((XS, BLOCK), 1) % XS == iota((XS, BLOCK), 0), 1.0, 0.0)
    weight = jnp.concatenate([mask * right[q : q + 1] for q in range(PROBES)], axis=0)
    high = weight.astype(BF16)
    low = (weight - high.astype(F32)).astype(BF16)
    weight = jnp.concatenate(
        [jnp.concatenate([high, high], axis=1), jnp.concatenate([low, low], axis=1)], axis=0
    )

    copies = []
    for slab in range(SLABS):
        out = jnp.dot(weight, parts[slab], preferred_element_type=F32)
        out = out[:BLOCK] + out[BLOCK:]
        result[:, slab] = out.reshape(PROBES, XS, YS)
        if slab % CHUNK == CHUNK - 1:
            span = pl.ds(slab - CHUNK + 1, CHUNK)
            copy = pltpu.make_async_copy(result.at[:, span], basis.at[:, span], sems.at[slab // CHUNK])
            copy.start()
            copies.append(copy)
        if slab == CHUNK:
            upper = jnp.where(lane // XS >= row, left * (root * (1.0 / scale)), 0.0)
            chosen = jnp.where(iota((BLOCK, PROBES), 0) == XS * iota((BLOCK, PROBES), 1), 1.0, 0.0)
            small[...] = jnp.dot(upper, chosen, precision=lax.Precision.HIGHEST, preferred_element_type=F32)
            copy = pltpu.make_async_copy(small, factor, sems.at[SLABS // CHUNK])
            copy.start()
            copies.append(copy)
    for copy in copies:
        copy.wait()


def orthonormal(parts, pieces, scale):
    whole = pl.BlockSpec(memory_space=pltpu.VMEM)
    return pl.pallas_call(
        functools.partial(basis_kernel, scale),
        out_shape=[
            jax.ShapeDtypeStruct((PROBES, SLABS, XS, YS), F32),
            jax.ShapeDtypeStruct((PROBES, PROBES), F32),
        ],
        in_specs=[whole, whole],
        out_specs=[pl.BlockSpec(memory_space=pl.ANY)] * 2,
        scratch_shapes=[
            pltpu.VMEM((PROBES, SLABS, XS, YS), F32),
            pltpu.VMEM((PROBES, PROBES), F32),
            pltpu.SemaphoreType.DMA((SLABS // CHUNK + 1,)),
        ],
        compiler_params=params(),
        name="orthonormal",
    )(parts, pieces)


def swap(array, axis, first):
    count = lax.axis_size(axis)
    pairs = [(i, i + 1) for i in range(0 if first else 1, count - 1, 2)]
    return lax.ppermute(array, axis, pairs + [(j, i) for i, j in pairs])


def all_copies(array, axes):
    copies = jnp.broadcast_to(array[None], (lax.axis_size(axes),) + array.shape)
    return lax.all_to_all(copies, axes, 0, 0)


def on_device(probes, material, visc_table, brink_table, cond_table, base_flow):
    shape = probes.shape
    probes = probes.reshape(PROBES, SLABS, XS, YS)
    x_first, x_second, y_first, y_second, wide, flow, visc, brink, cond, along_y, along_x, ends_at = load(
        probes, material, base_flow, (visc_table, brink_table, cond_table)
    )
    x_second = swap(x_second, GX, False)
    x_first = swap(x_first, GX, True)
    y_second = swap(y_second, GY, False)
    y_first = swap(y_first, GY, True)
    halos = (x_second, x_first, y_second, y_first)
    image = inner(wide, flow, visc, brink, cond, along_y, along_x)
    parts, local = gram(image, visc, cond, ends_at, halos)
    slab_sum = jnp.sum(all_copies(local, ("core", "y")), axis=0)
    pieces = all_copies(slab_sum, ("z", "x"))
    rows_total = SLABS * XS * YS * lax.axis_size(GX) * lax.axis_size(GY)
    basis, factor = orthonormal(parts, pieces, math.sqrt(rows_total))
    return (basis.reshape(shape), factor)


def solution(mesh):
    rows, columns = mesh.shape["gx"], mesh.shape["gy"]
    wide, cores = (4 if rows % 4 == 0 else 1), (2 if columns % 2 == 0 else 1)
    mesh = jax.sharding.Mesh(
        mesh.devices.reshape(rows // wide, wide, columns // cores, cores), ("y", "x", "z", "core")
    )
    grid = P(None, GX, GY)
    in_specs = (P(None, None, None, GX, GY), grid, P(), P(), P(), grid)
    out_specs = (P(None, None, None, GX, GY), P())
    return jax.shard_map(
        on_device, mesh=mesh, in_specs=in_specs, out_specs=out_specs, check_vma=False
    )
```

```python
import functools
import math

import jax
import jax.numpy as jnp
from jax import lax
from jax.experimental import pallas as pl
from jax.experimental.pallas import tpu as pltpu
from jax.sharding import PartitionSpec as P

GX = ("y", "x")
GY = ("z", "core")
PROBES = 16
SLABS = 24
DEPTH = 12
XS = 8
YS = 256
BLOCK = PROBES * XS
F32 = jnp.float32
BF16 = jnp.bfloat16
NT = (((1,), (1,)), ((), ()))


def iota(shape, dim):
    return lax.broadcasted_iota(jnp.int32, shape, dim)


def params():
    return pltpu.CompilerParams(vmem_limit_bytes=24 * 1024 * 1024)


def pick(material, table):
    value = jnp.where(material == 0, table[0], table[1])
    value = jnp.where(material == 2, table[2], value)
    return jnp.where(material == 3, table[3], value)


def first_ends(parity):
    return (XS - 1) * (1 - parity[0]), (YS - 1) * (1 - parity[1])


def parities():
    return lax.axis_index(GX) % 2, lax.axis_index(GY) % 2


LOADS = 4


def whole_rows(wide, slab):
    return jnp.concatenate([wide[0, slab], wide[1, slab]], axis=1)


def load_kernel(
    probes, material, flow_in, visc_in, brink_in, cond_in,
    x_first, x_second, y_first, y_second, wide, flow, visc, brink, cond, along_y, along_x, ends_at,
    kind, tables, packed, columns, sems,
):
    each = PROBES // LOADS
    loads = [
        pltpu.make_async_copy(probes.at[pl.ds(i * each, each)], packed.at[pl.ds(i * each, each)], sems.at[i])
        for i in range(LOADS)
    ]
    others = ((material, kind), (visc_in, tables.at[0]), (brink_in, tables.at[1]), (cond_in, tables.at[2]), (flow_in, flow))
    others = [pltpu.make_async_copy(src, dst, sems.at[LOADS + i]) for i, (src, dst) in enumerate(others)]
    for copy in loads + others:
        copy.start()
    x_end, y_end = first_ends(parities())
    row, lane = iota((YS, YS), 0), iota((YS, YS), 1)
    along_y[...] = jnp.where(row == lane, 6.0, jnp.where(jnp.abs(row - lane) == 1, -1.0, 0.0)).astype(BF16)
    along_x[...] = jnp.where((jnp.abs(row - lane) == 1) & (row // XS == lane // XS), -1.0, 0.0).astype(BF16)
    row, lane = iota((64, YS), 0), iota((64, YS), 1)
    at_end = jnp.where(row < 32, y_end, YS - 1 - y_end) == lane
    for slab in range(SLABS):
        ends_at[slab] = jnp.where(at_end & (row % 32 == slab), 1.0, 0.0).astype(BF16)
    lane = iota((XS, 128), 1)
    for i, copy in enumerate(loads):
        copy.wait()
        for probe in range(i * each, (i + 1) * each):
            field = packed[probe].astype(F32)
            rows = slice(probe * XS, (probe + 1) * XS)
            wide[0, :, rows, :] = field[:, :, :128]
            wide[1, :, rows, :] = field[:, :, 128:]
            ends = jnp.where(lane < 64, field[:, :, :128], field[:, :, 128:])
            sides = jnp.zeros((XS, 128), F32)
            for slab in range(SLABS):
                sides = jnp.where(lane // 2 == slab, pltpu.roll(ends[slab], 2 * slab + 1, 1), sides)
            columns[rows] = sides
    x_faces(wide, x_end, x_first, x_second)
    columns[...] = columns[...].T
    high, low = columns[pl.ds(0, 32, stride=2), :], columns[pl.ds(1, 32, stride=2), :]
    y_first[...] = jnp.where(y_end == 0, low, high).astype(BF16)
    y_second[...] = jnp.where(y_end == 0, high, low).astype(BF16)
    for copy in others:
        copy.wait()
    for i, value in enumerate((visc, brink, cond)):
        value[...] = pick(kind[...], [tables[i, j] for j in range(4)])


def x_faces(wide, x_end, x_first, x_second):
    rows = wide.reshape(2, SLABS * BLOCK, 128)
    for half in range(2):
        span = slice(half * 128, half * 128 + 128)
        low = rows[half, pl.ds(0, SLABS * PROBES, stride=XS), :]
        high = rows[half, pl.ds(XS - 1, SLABS * PROBES, stride=XS), :]
        x_first[:, span] = jnp.where(x_end == 0, low, high).astype(BF16)
        x_second[:, span] = jnp.where(x_end == 0, high, low).astype(BF16)


def load(probes, material, flow, tables):
    cells = (DEPTH, XS, YS)
    arrays = [pltpu.with_memory_space_constraint(a, pltpu.HBM) for a in (probes, material, flow, *tables)]
    whole = pl.BlockSpec(memory_space=pltpu.VMEM)
    return pl.pallas_call(
        load_kernel,
        out_shape=[pltpu.VMEM((SLABS * PROBES, YS), BF16)] * 2
        + [pltpu.VMEM((32, BLOCK), BF16)] * 2
        + [pltpu.VMEM((2, SLABS, BLOCK, 128), F32)]
        + [pltpu.VMEM(cells, F32)] * 4
        + [pltpu.VMEM((YS, YS), BF16)] * 2
        + [pltpu.VMEM((SLABS, 64, YS), BF16)],
        in_specs=[pl.BlockSpec(memory_space=pl.ANY)] * 6,
        out_specs=[whole] * 12,
        scratch_shapes=[
            pltpu.VMEM(cells, jnp.int32),
            pltpu.SMEM((3, 4), F32),
            pltpu.VMEM((PROBES, SLABS, XS, YS), BF16),
            pltpu.VMEM((BLOCK, 128), F32),
            pltpu.SemaphoreType.DMA((LOADS + 5,)),
        ],
        compiler_params=params(),
        name="load",
    )(*arrays)


def inner_kernel(wide, flow, visc, brink, cond, along_y, along_x, image):
    block = (PROBES, XS, YS)

    def around(z):
        if z == 0:
            return whole_rows(wide, 1)
        if z == DEPTH - 1:
            return whole_rows(wide, z - 1)
        return whole_rows(wide, z - 1) + whole_rows(wide, z + 1)

    def around_t(z):
        if z == 0:
            return whole_rows(wide, DEPTH + 1)
        if z == DEPTH - 1:
            return whole_rows(wide, DEPTH + z - 1)
        return whole_rows(wide, DEPTH + z - 1) + whole_rows(wide, DEPTH + z + 1)

    for z in range(DEPTH):
        w, t = whole_rows(wide, z), whole_rows(wide, DEPTH + z)
        both = jnp.concatenate([w.astype(BF16), t.astype(BF16)], axis=0)
        lap = jnp.dot(both, along_y[...], preferred_element_type=F32)
        lap = lap + jnp.dot(along_x[...], both, preferred_element_type=F32)
        w_lap = (lap[:BLOCK] - around(z)).reshape(block)
        t_lap = (lap[BLOCK:] - around_t(z)).reshape(block)
        w3, t3 = w.reshape(block), t.reshape(block)
        rise = t3 if z == 0 else t3 - whole_rows(wide, DEPTH + z - 1).reshape(block)
        image[z] = (visc[z][None] * w_lap + brink[z][None] * w3 - t3).reshape(BLOCK, YS)
        image[DEPTH + z] = (cond[z][None] * t_lap + 0.5 * w3 + flow[z][None] * rise).reshape(BLOCK, YS)


def inner(*arrays):
    whole = pl.BlockSpec(memory_space=pltpu.VMEM)
    return pl.pallas_call(
        inner_kernel,
        out_shape=pltpu.VMEM((SLABS, BLOCK, YS), F32),
        in_specs=[whole] * 7,
        out_specs=whole,
        compiler_params=params(),
        cost_estimate=pl.CostEstimate(flops=800_000_000, bytes_accessed=6_000_000, transcendentals=0),
        name="inner",
    )(*arrays)


def fold_lanes(half):
    lane = iota((8, BLOCK), 1)
    for step in (1, 2):
        ahead = pltpu.roll(half, BLOCK - step, 1)
        behind = pltpu.roll(half, step, 1)
        half = half + jnp.where(lane & step == 0, ahead, behind)
    return half


def gram_kernel(image, visc, cond, ends_at, x_second, x_first, y_second, y_first, parts, gram, total):
    x_end, _ = first_ends(parities())
    row, lane = iota((BLOCK, 2 * PROBES), 0), iota((BLOCK, 2 * PROBES), 1)
    target = jnp.where(lane < PROBES, x_end, XS - 1 - x_end)
    place = jnp.where((row % XS == target) & (row // XS == lane % PROBES), 1.0, 0.0).astype(BF16)
    columns = jnp.concatenate([y_first[...].astype(F32), y_second[...].astype(F32)], axis=0).T
    place = jnp.concatenate([place, columns.astype(BF16)], axis=1)
    for slab in range(SLABS):
        factor = visc[slab] if slab < DEPTH else cond[slab - DEPTH]
        span = pl.ds(slab * PROBES, PROBES)
        edges = jnp.concatenate([x_first[span, :], x_second[span, :], ends_at[slab]], axis=0)
        halo = jnp.dot(place, edges, preferred_element_type=F32).reshape(PROBES, XS, YS)
        full = image[slab] - (factor[None] * halo).reshape(BLOCK, YS)
        high = full.astype(BF16)
        parts[slab, :BLOCK] = high
        parts[slab, BLOCK:] = (full - high.astype(F32)).astype(BF16)
    for slab in range(SLABS):
        product = lax.dot_general(parts[slab], parts[slab, :BLOCK], NT, preferred_element_type=F32)
        if slab == 0:
            total[...] = product
        else:
            total[...] += product
    mixed = total[BLOCK:]
    square = total[:BLOCK] + mixed + mixed.T
    row, lane = iota((BLOCK, BLOCK), 0), iota((BLOCK, BLOCK), 1)
    square = jnp.where(row % XS == lane % XS, square, 0.0)
    square = jnp.sum(square.reshape(PROBES, XS, BLOCK), axis=1)
    top, bottom = square[:8], square[8:]
    first = iota((8, BLOCK), 1) % XS < XS // 2
    top = top + pltpu.roll(top, BLOCK - XS // 2, 1)
    bottom = bottom + pltpu.roll(bottom, XS // 2, 1)
    half = fold_lanes(jnp.where(first, top, bottom))
    half = jnp.where(iota((8, BLOCK), 1) % 4 == iota((8, BLOCK), 0) % 4, half, 0.0)
    half = half + pltpu.roll(half, 7, 0)
    half = half + pltpu.roll(half, 6, 0)
    gram[:, :BLOCK] = half[:1]
    gram[:, BLOCK:] = half[4:5]


def gram(image, visc, cond, ends_at, halos):
    whole = pl.BlockSpec(memory_space=pltpu.VMEM)
    return pl.pallas_call(
        gram_kernel,
        out_shape=[
            pltpu.VMEM((SLABS, 2 * BLOCK, YS), BF16),
            jax.ShapeDtypeStruct((1, 2 * BLOCK), F32),
        ],
        in_specs=[whole] * 8,
        out_specs=[whole] * 2,
        scratch_shapes=[pltpu.VMEM((2 * BLOCK, BLOCK), F32)],
        compiler_params=params(),
        name="gram",
    )(image, visc, cond, ends_at, *halos)


CHUNK = 4


def basis_kernel(scale, parts, pieces, basis, factor, result, small, sems):
    shape = (PROBES, BLOCK)
    row, lane = iota(shape, 0), iota(shape, 1)
    both = jnp.sum(pieces[...], axis=0)
    lane8, row8 = iota((8, BLOCK), 1), iota((8, BLOCK), 0)
    half = jnp.where(
        row8 < 4, jnp.broadcast_to(both[:, :BLOCK], (8, BLOCK)), jnp.broadcast_to(both[:, BLOCK:], (8, BLOCK))
    )
    half = fold_lanes(jnp.where(lane8 % 4 == row8 % 4, half, 0.0))
    first = lane8 % XS < XS // 2
    top = jnp.where(first, half, pltpu.roll(half, XS // 2, 1))
    bottom = jnp.where(first, pltpu.roll(half, BLOCK - XS // 2, 1), half)
    left = jnp.concatenate([top, bottom], axis=0)
    right = jnp.where(lane // XS == row, 1.0, 0.0).astype(F32)
    heads, crosses, tails = (jnp.ones(shape, F32) for _ in range(3))
    columns = [jnp.broadcast_to(left[:, k * XS : k * XS + 1], shape) for k in range(PROBES)]
    for k in range(0, PROBES, 2):
        one, two = columns[k : k + 2]
        head = jnp.broadcast_to(one[k : k + 1], shape)
        cross = jnp.broadcast_to(one[k + 1 : k + 2], shape)
        tail = jnp.broadcast_to(two[k + 1 : k + 2], shape)
        mine = row // 2 == k // 2
        heads = jnp.where(mine, head, heads)
        crosses = jnp.where(mine, cross, crosses)
        tails = jnp.where(mine, tail, tails)
        if k + 2 < PROBES:
            inverse = 1.0 / head
            lean = cross * inverse
            over = jnp.where(row > k + 1, 1.0 / (tail - lean * cross), 0.0)
            second_ratio = (two - lean * one) * over
            first_ratio = jnp.where(row > k + 1, one * inverse, 0.0) - lean * second_ratio
            for j in range(k + 2, PROBES):
                columns[j] = (
                    columns[j]
                    - first_ratio * jnp.broadcast_to(one[j : j + 1], shape)
                    - second_ratio * jnp.broadcast_to(two[j : j + 1], shape)
                )
            left, right = (
                side
                - first_ratio * jnp.broadcast_to(side[k : k + 1], shape)
                - second_ratio * jnp.broadcast_to(side[k + 1 : k + 2], shape)
                for side in (left, right)
            )
    odd = row % 2 == 1
    ratio = jnp.where(odd, crosses / heads, 0.0)
    left, right = (side - ratio * pltpu.roll(side, 1, 0) for side in (left, right))
    pivots = jnp.where(odd, tails - ratio * crosses, heads)
    root = lax.rsqrt(pivots)
    root = root * (1.5 - 0.5 * pivots * root * root)
    right = right * (root * scale)
    mask = jnp.where(iota((XS, BLOCK), 1) % XS == iota((XS, BLOCK), 0), 1.0, 0.0)
    weight = jnp.concatenate([mask * right[q : q + 1] for q in range(PROBES)], axis=0)
    high = weight.astype(BF16)
    low = (weight - high.astype(F32)).astype(BF16)
    weight = jnp.concatenate(
        [jnp.concatenate([high, high], axis=1), jnp.concatenate([low, low], axis=1)], axis=0
    )

    copies = []
    for slab in range(SLABS):
        out = jnp.dot(weight, parts[slab], preferred_element_type=F32)
        out = out[:BLOCK] + out[BLOCK:]
        result[:, slab] = out.reshape(PROBES, XS, YS)
        if slab % CHUNK == CHUNK - 1:
            span = pl.ds(slab - CHUNK + 1, CHUNK)
            copy = pltpu.make_async_copy(result.at[:, span], basis.at[:, span], sems.at[slab // CHUNK])
            copy.start()
            copies.append(copy)
        if slab == CHUNK:
            upper = jnp.where(lane // XS >= row, left * (root * (1.0 / scale)), 0.0)
            chosen = jnp.where(iota((BLOCK, PROBES), 0) == XS * iota((BLOCK, PROBES), 1), 1.0, 0.0)
            small[...] = jnp.dot(upper, chosen, precision=lax.Precision.HIGHEST, preferred_element_type=F32)
            copy = pltpu.make_async_copy(small, factor, sems.at[SLABS // CHUNK])
            copy.start()
            copies.append(copy)
    for copy in copies:
        copy.wait()


def orthonormal(parts, pieces, scale):
    whole = pl.BlockSpec(memory_space=pltpu.VMEM)
    return pl.pallas_call(
        functools.partial(basis_kernel, scale),
        out_shape=[
            jax.ShapeDtypeStruct((PROBES, SLABS, XS, YS), F32),
            jax.ShapeDtypeStruct((PROBES, PROBES), F32),
        ],
        in_specs=[whole, whole],
        out_specs=[pl.BlockSpec(memory_space=pl.ANY)] * 2,
        scratch_shapes=[
            pltpu.VMEM((PROBES, SLABS, XS, YS), F32),
            pltpu.VMEM((PROBES, PROBES), F32),
            pltpu.SemaphoreType.DMA((SLABS // CHUNK + 1,)),
        ],
        compiler_params=params(),
        name="orthonormal",
    )(parts, pieces)


def swap(array, axis, first):
    count = lax.axis_size(axis)
    pairs = [(i, i + 1) for i in range(0 if first else 1, count - 1, 2)]
    return lax.ppermute(array, axis, pairs + [(j, i) for i, j in pairs])


def all_copies(array, axes):
    copies = jnp.broadcast_to(array[None], (lax.axis_size(axes),) + array.shape)
    return lax.all_to_all(copies, axes, 0, 0)


def on_device(probes, material, visc_table, brink_table, cond_table, base_flow):
    shape = probes.shape
    probes = probes.reshape(PROBES, SLABS, XS, YS)
    x_first, x_second, y_first, y_second, wide, flow, visc, brink, cond, along_y, along_x, ends_at = load(
        probes, material, base_flow, (visc_table, brink_table, cond_table)
    )
    x_second = swap(x_second, GX, False)
    x_first = swap(x_first, GX, True)
    y_second = swap(y_second, GY, False)
    y_first = swap(y_first, GY, True)
    halos = (x_second, x_first, y_second, y_first)
    image = inner(wide, flow, visc, brink, cond, along_y, along_x)
    parts, local = gram(image, visc, cond, ends_at, halos)
    slab_sum = jnp.sum(all_copies(local, ("core", "y")), axis=0)
    pieces = all_copies(slab_sum, ("z", "x"))
    rows_total = SLABS * XS * YS * lax.axis_size(GX) * lax.axis_size(GY)
    basis, factor = orthonormal(parts, pieces, math.sqrt(rows_total))
    return (basis.reshape(shape), factor)


def solution(mesh):
    rows, columns = mesh.shape["gx"], mesh.shape["gy"]
    wide, cores = (4 if rows % 4 == 0 else 1), (2 if columns % 2 == 0 else 1)
    mesh = jax.sharding.Mesh(
        mesh.devices.reshape(rows // wide, wide, columns // cores, cores), ("y", "x", "z", "core")
    )
    grid = P(None, GX, GY)
    in_specs = (P(None, None, None, GX, GY), grid, P(), P(), P(), grid)
    out_specs = (P(None, None, None, GX, GY), P())
    return jax.shard_map(
        on_device, mesh=mesh, in_specs=in_specs, out_specs=out_specs, check_vma=False
    )
```

```python
import functools
import math

import jax
import jax.numpy as jnp
from jax import lax
from jax.experimental import pallas as pl
from jax.experimental.pallas import tpu as pltpu
from jax.sharding import PartitionSpec as P

GX = ("y", "x")
GY = ("z", "core")
PROBES = 16
SLABS = 24
DEPTH = 12
XS = 8
YS = 256
BLOCK = PROBES * XS
F32 = jnp.float32
BF16 = jnp.bfloat16
NT = (((1,), (1,)), ((), ()))


def iota(shape, dim):
    return lax.broadcasted_iota(jnp.int32, shape, dim)


def params():
    return pltpu.CompilerParams(vmem_limit_bytes=24 * 1024 * 1024)


def pick(material, table):
    value = jnp.where(material == 0, table[0], table[1])
    value = jnp.where(material == 2, table[2], value)
    return jnp.where(material == 3, table[3], value)


def first_ends(parity):
    return (XS - 1) * (1 - parity[0]), (YS - 1) * (1 - parity[1])


def parities():
    return lax.axis_index(GX) % 2, lax.axis_index(GY) % 2


LOADS = 4


def whole_rows(wide, slab):
    return jnp.concatenate([wide[0, slab], wide[1, slab]], axis=1)


def load_kernel(
    probes, material, flow_in, visc_in, brink_in, cond_in,
    x_first, x_second, y_first, y_second, wide, flow, visc, brink, cond, along_y, along_x, ends_at,
    kind, tables, packed, columns, sems,
):
    each = PROBES // LOADS
    loads = [
        pltpu.make_async_copy(probes.at[pl.ds(i * each, each)], packed.at[pl.ds(i * each, each)], sems.at[i])
        for i in range(LOADS)
    ]
    others = ((material, kind), (visc_in, tables.at[0]), (brink_in, tables.at[1]), (cond_in, tables.at[2]), (flow_in, flow))
    others = [pltpu.make_async_copy(src, dst, sems.at[LOADS + i]) for i, (src, dst) in enumerate(others)]
    for copy in loads + others:
        copy.start()
    x_end, y_end = first_ends(parities())
    row, lane = iota((YS, YS), 0), iota((YS, YS), 1)
    along_y[...] = jnp.where(row == lane, 6.0, jnp.where(jnp.abs(row - lane) == 1, -1.0, 0.0)).astype(BF16)
    along_x[...] = jnp.where((jnp.abs(row - lane) == 1) & (row // XS == lane // XS), -1.0, 0.0).astype(BF16)
    row, lane = iota((64, YS), 0), iota((64, YS), 1)
    at_end = jnp.where(row < 32, y_end, YS - 1 - y_end) == lane
    for slab in range(SLABS):
        ends_at[slab] = jnp.where(at_end & (row % 32 == slab), 1.0, 0.0).astype(BF16)
    lane = iota((XS, 128), 1)
    for i, copy in enumerate(loads):
        copy.wait()
        for probe in range(i * each, (i + 1) * each):
            field = packed[probe].astype(F32)
            rows = slice(probe * XS, (probe + 1) * XS)
            wide[0, :, rows, :] = field[:, :, :128]
            wide[1, :, rows, :] = field[:, :, 128:]
            ends = jnp.where(lane < 64, field[:, :, :128], field[:, :, 128:])
            sides = jnp.zeros((XS, 128), F32)
            for slab in range(SLABS):
                sides = jnp.where(lane // 2 == slab, pltpu.roll(ends[slab], 2 * slab + 1, 1), sides)
            columns[rows] = sides
    x_faces(wide, x_end, x_first, x_second)
    columns[...] = columns[...].T
    high, low = columns[pl.ds(0, 32, stride=2), :], columns[pl.ds(1, 32, stride=2), :]
    y_first[...] = jnp.where(y_end == 0, low, high).astype(BF16)
    y_second[...] = jnp.where(y_end == 0, high, low).astype(BF16)
    for copy in others:
        copy.wait()
    for i, value in enumerate((visc, brink, cond)):
        value[...] = pick(kind[...], [tables[i, j] for j in range(4)])


def x_faces(wide, x_end, x_first, x_second):
    rows = wide.reshape(2, SLABS * BLOCK, 128)
    for half in range(2):
        span = slice(half * 128, half * 128 + 128)
        low = rows[half, pl.ds(0, SLABS * PROBES, stride=XS), :]
        high = rows[half, pl.ds(XS - 1, SLABS * PROBES, stride=XS), :]
        x_first[:, span] = jnp.where(x_end == 0, low, high).astype(BF16)
        x_second[:, span] = jnp.where(x_end == 0, high, low).astype(BF16)


def load(probes, material, flow, tables):
    cells = (DEPTH, XS, YS)
    arrays = [pltpu.with_memory_space_constraint(a, pltpu.HBM) for a in (probes, material, flow, *tables)]
    whole = pl.BlockSpec(memory_space=pltpu.VMEM)
    return pl.pallas_call(
        load_kernel,
        out_shape=[pltpu.VMEM((SLABS * PROBES, YS), BF16)] * 2
        + [pltpu.VMEM((32, BLOCK), BF16)] * 2
        + [pltpu.VMEM((2, SLABS, BLOCK, 128), F32)]
        + [pltpu.VMEM(cells, F32)] * 4
        + [pltpu.VMEM((YS, YS), BF16)] * 2
        + [pltpu.VMEM((SLABS, 64, YS), BF16)],
        in_specs=[pl.BlockSpec(memory_space=pl.ANY)] * 6,
        out_specs=[whole] * 12,
        scratch_shapes=[
            pltpu.VMEM(cells, jnp.int32),
            pltpu.SMEM((3, 4), F32),
            pltpu.VMEM((PROBES, SLABS, XS, YS), BF16),
            pltpu.VMEM((BLOCK, 128), F32),
            pltpu.SemaphoreType.DMA((LOADS + 5,)),
        ],
        compiler_params=params(),
        name="load",
    )(*arrays)


def inner_kernel(wide, flow, visc, brink, cond, along_y, along_x, image):
    block = (PROBES, XS, YS)

    def around(z):
        if z == 0:
            return whole_rows(wide, 1)
        if z == DEPTH - 1:
            return whole_rows(wide, z - 1)
        return whole_rows(wide, z - 1) + whole_rows(wide, z + 1)

    def around_t(z):
        if z == 0:
            return whole_rows(wide, DEPTH + 1)
        if z == DEPTH - 1:
            return whole_rows(wide, DEPTH + z - 1)
        return whole_rows(wide, DEPTH + z - 1) + whole_rows(wide, DEPTH + z + 1)

    for z in range(DEPTH):
        w, t = whole_rows(wide, z), whole_rows(wide, DEPTH + z)
        both = jnp.concatenate([w.astype(BF16), t.astype(BF16)], axis=0)
        lap = jnp.dot(both, along_y[...], preferred_element_type=F32)
        lap = lap + jnp.dot(along_x[...], both, preferred_element_type=F32)
        w_lap = (lap[:BLOCK] - around(z)).reshape(block)
        t_lap = (lap[BLOCK:] - around_t(z)).reshape(block)
        w3, t3 = w.reshape(block), t.reshape(block)
        rise = t3 if z == 0 else t3 - whole_rows(wide, DEPTH + z - 1).reshape(block)
        image[z] = (visc[z][None] * w_lap + brink[z][None] * w3 - t3).reshape(BLOCK, YS)
        image[DEPTH + z] = (cond[z][None] * t_lap + 0.5 * w3 + flow[z][None] * rise).reshape(BLOCK, YS)


def inner(*arrays):
    whole = pl.BlockSpec(memory_space=pltpu.VMEM)
    return pl.pallas_call(
        inner_kernel,
        out_shape=pltpu.VMEM((SLABS, BLOCK, YS), F32),
        in_specs=[whole] * 7,
        out_specs=whole,
        compiler_params=params(),
        cost_estimate=pl.CostEstimate(flops=800_000_000, bytes_accessed=6_000_000, transcendentals=0),
        name="inner",
    )(*arrays)


def fold_lanes(half):
    lane = iota((8, BLOCK), 1)
    for step in (1, 2):
        ahead = pltpu.roll(half, BLOCK - step, 1)
        behind = pltpu.roll(half, step, 1)
        half = half + jnp.where(lane & step == 0, ahead, behind)
    return half


def gram_kernel(image, visc, cond, ends_at, x_second, x_first, y_second, y_first, parts, gram, total):
    x_end, _ = first_ends(parities())
    row, lane = iota((BLOCK, 2 * PROBES), 0), iota((BLOCK, 2 * PROBES), 1)
    target = jnp.where(lane < PROBES, x_end, XS - 1 - x_end)
    place = jnp.where((row % XS == target) & (row // XS == lane % PROBES), 1.0, 0.0).astype(BF16)
    columns = jnp.concatenate([y_first[...].astype(F32), y_second[...].astype(F32)], axis=0).T
    place = jnp.concatenate([place, columns.astype(BF16)], axis=1)
    for slab in range(SLABS):
        factor = visc[slab] if slab < DEPTH else cond[slab - DEPTH]
        span = pl.ds(slab * PROBES, PROBES)
        edges = jnp.concatenate([x_first[span, :], x_second[span, :], ends_at[slab]], axis=0)
        halo = jnp.dot(place, edges, preferred_element_type=F32).reshape(PROBES, XS, YS)
        full = image[slab] - (factor[None] * halo).reshape(BLOCK, YS)
        high = full.astype(BF16)
        parts[slab, :BLOCK] = high
        parts[slab, BLOCK:] = (full - high.astype(F32)).astype(BF16)
    for slab in range(SLABS):
        product = lax.dot_general(parts[slab], parts[slab, :BLOCK], NT, preferred_element_type=F32)
        if slab == 0:
            total[...] = product
        else:
            total[...] += product
    mixed = total[BLOCK:]
    square = total[:BLOCK] + mixed + mixed.T
    row, lane = iota((BLOCK, BLOCK), 0), iota((BLOCK, BLOCK), 1)
    square = jnp.where(row % XS == lane % XS, square, 0.0)
    square = jnp.sum(square.reshape(PROBES, XS, BLOCK), axis=1)
    top, bottom = square[:8], square[8:]
    first = iota((8, BLOCK), 1) % XS < XS // 2
    top = top + pltpu.roll(top, BLOCK - XS // 2, 1)
    bottom = bottom + pltpu.roll(bottom, XS // 2, 1)
    half = fold_lanes(jnp.where(first, top, bottom))
    half = jnp.where(iota((8, BLOCK), 1) % 4 == iota((8, BLOCK), 0) % 4, half, 0.0)
    half = half + pltpu.roll(half, 7, 0)
    half = half + pltpu.roll(half, 6, 0)
    gram[:, :BLOCK] = half[:1]
    gram[:, BLOCK:] = half[4:5]


def gram(image, visc, cond, ends_at, halos):
    whole = pl.BlockSpec(memory_space=pltpu.VMEM)
    return pl.pallas_call(
        gram_kernel,
        out_shape=[
            pltpu.VMEM((SLABS, 2 * BLOCK, YS), BF16),
            jax.ShapeDtypeStruct((1, 2 * BLOCK), F32),
        ],
        in_specs=[whole] * 8,
        out_specs=[whole] * 2,
        scratch_shapes=[pltpu.VMEM((2 * BLOCK, BLOCK), F32)],
        compiler_params=params(),
        name="gram",
    )(image, visc, cond, ends_at, *halos)


CHUNK = 4


def basis_kernel(scale, parts, pieces, basis, factor, result, small, sems):
    shape = (PROBES, BLOCK)
    row, lane = iota(shape, 0), iota(shape, 1)
    both = jnp.sum(pieces[...], axis=0)
    lane8, row8 = iota((8, BLOCK), 1), iota((8, BLOCK), 0)
    half = jnp.where(
        row8 < 4, jnp.broadcast_to(both[:, :BLOCK], (8, BLOCK)), jnp.broadcast_to(both[:, BLOCK:], (8, BLOCK))
    )
    half = fold_lanes(jnp.where(lane8 % 4 == row8 % 4, half, 0.0))
    first = lane8 % XS < XS // 2
    top = jnp.where(first, half, pltpu.roll(half, XS // 2, 1))
    bottom = jnp.where(first, pltpu.roll(half, BLOCK - XS // 2, 1), half)
    left = jnp.concatenate([top, bottom], axis=0)
    right = jnp.where(lane // XS == row, 1.0, 0.0).astype(F32)
    heads, crosses, tails = (jnp.ones(shape, F32) for _ in range(3))
    columns = [jnp.broadcast_to(left[:, k * XS : k * XS + 1], shape) for k in range(PROBES)]
    for k in range(0, PROBES, 2):
        one, two = columns[k : k + 2]
        head = jnp.broadcast_to(one[k : k + 1], shape)
        cross = jnp.broadcast_to(one[k + 1 : k + 2], shape)
        tail = jnp.broadcast_to(two[k + 1 : k + 2], shape)
        mine = row // 2 == k // 2
        heads = jnp.where(mine, head, heads)
        crosses = jnp.where(mine, cross, crosses)
        tails = jnp.where(mine, tail, tails)
        if k + 2 < PROBES:
            inverse = 1.0 / head
            lean = cross * inverse
            over = jnp.where(row > k + 1, 1.0 / (tail - lean * cross), 0.0)
            second_ratio = (two - lean * one) * over
            first_ratio = jnp.where(row > k + 1, one * inverse, 0.0) - lean * second_ratio
            for j in range(k + 2, PROBES):
                columns[j] = (
                    columns[j]
                    - first_ratio * jnp.broadcast_to(one[j : j + 1], shape)
                    - second_ratio * jnp.broadcast_to(two[j : j + 1], shape)
                )
            left, right = (
                side
                - first_ratio * jnp.broadcast_to(side[k : k + 1], shape)
                - second_ratio * jnp.broadcast_to(side[k + 1 : k + 2], shape)
                for side in (left, right)
            )
    odd = row % 2 == 1
    ratio = jnp.where(odd, crosses / heads, 0.0)
    left, right = (side - ratio * pltpu.roll(side, 1, 0) for side in (left, right))
    pivots = jnp.where(odd, tails - ratio * crosses, heads)
    root = lax.rsqrt(pivots)
    root = root * (1.5 - 0.5 * pivots * root * root)
    right = right * (root * scale)
    mask = jnp.where(iota((XS, BLOCK), 1) % XS == iota((XS, BLOCK), 0), 1.0, 0.0)
    weight = jnp.concatenate([mask * right[q : q + 1] for q in range(PROBES)], axis=0)
    high = weight.astype(BF16)
    low = (weight - high.astype(F32)).astype(BF16)
    weight = jnp.concatenate(
        [jnp.concatenate([high, high], axis=1), jnp.concatenate([low, low], axis=1)], axis=0
    )

    copies = []
    for slab in range(SLABS):
        out = jnp.dot(weight, parts[slab], preferred_element_type=F32)
        out = out[:BLOCK] + out[BLOCK:]
        result[:, slab] = out.reshape(PROBES, XS, YS)
        if slab % CHUNK == CHUNK - 1:
            span = pl.ds(slab - CHUNK + 1, CHUNK)
            copy = pltpu.make_async_copy(result.at[:, span], basis.at[:, span], sems.at[slab // CHUNK])
            copy.start()
            copies.append(copy)
        if slab == CHUNK:
            upper = jnp.where(lane // XS >= row, left * (root * (1.0 / scale)), 0.0)
            chosen = jnp.where(iota((BLOCK, PROBES), 0) == XS * iota((BLOCK, PROBES), 1), 1.0, 0.0)
            small[...] = jnp.dot(upper, chosen, precision=lax.Precision.HIGHEST, preferred_element_type=F32)
            copy = pltpu.make_async_copy(small, factor, sems.at[SLABS // CHUNK])
            copy.start()
            copies.append(copy)
    for copy in copies:
        copy.wait()


def orthonormal(parts, pieces, scale):
    whole = pl.BlockSpec(memory_space=pltpu.VMEM)
    return pl.pallas_call(
        functools.partial(basis_kernel, scale),
        out_shape=[
            jax.ShapeDtypeStruct((PROBES, SLABS, XS, YS), F32),
            jax.ShapeDtypeStruct((PROBES, PROBES), F32),
        ],
        in_specs=[whole, whole],
        out_specs=[pl.BlockSpec(memory_space=pl.ANY)] * 2,
        scratch_shapes=[
            pltpu.VMEM((PROBES, SLABS, XS, YS), F32),
            pltpu.VMEM((PROBES, PROBES), F32),
            pltpu.SemaphoreType.DMA((SLABS // CHUNK + 1,)),
        ],
        compiler_params=params(),
        name="orthonormal",
    )(parts, pieces)


def swap(array, axis, first):
    count = lax.axis_size(axis)
    pairs = [(i, i + 1) for i in range(0 if first else 1, count - 1, 2)]
    return lax.ppermute(array, axis, pairs + [(j, i) for i, j in pairs])


def all_copies(array, axes):
    copies = jnp.broadcast_to(array[None], (lax.axis_size(axes),) + array.shape)
    return lax.all_to_all(copies, axes, 0, 0)


def on_device(probes, material, visc_table, brink_table, cond_table, base_flow):
    shape = probes.shape
    probes = probes.reshape(PROBES, SLABS, XS, YS)
    x_first, x_second, y_first, y_second, wide, flow, visc, brink, cond, along_y, along_x, ends_at = load(
        probes, material, base_flow, (visc_table, brink_table, cond_table)
    )
    x_second = swap(x_second, GX, False)
    x_first = swap(x_first, GX, True)
    y_second = swap(y_second, GY, False)
    y_first = swap(y_first, GY, True)
    halos = (x_second, x_first, y_second, y_first)
    image = inner(wide, flow, visc, brink, cond, along_y, along_x)
    parts, local = gram(image, visc, cond, ends_at, halos)
    slab_sum = jnp.sum(all_copies(local, ("core", "z")), axis=0)
    pieces = all_copies(slab_sum, ("y", "x"))
    rows_total = SLABS * XS * YS * lax.axis_size(GX) * lax.axis_size(GY)
    basis, factor = orthonormal(parts, pieces, math.sqrt(rows_total))
    return (basis.reshape(shape), factor)


def solution(mesh):
    rows, columns = mesh.shape["gx"], mesh.shape["gy"]
    wide, cores = (4 if rows % 4 == 0 else 1), (2 if columns % 2 == 0 else 1)
    mesh = jax.sharding.Mesh(
        mesh.devices.reshape(rows // wide, wide, columns // cores, cores), ("y", "x", "z", "core")
    )
    grid = P(None, GX, GY)
    in_specs = (P(None, None, None, GX, GY), grid, P(), P(), P(), grid)
    out_specs = (P(None, None, None, GX, GY), P())
    return jax.shard_map(
        on_device, mesh=mesh, in_specs=in_specs, out_specs=out_specs, check_vma=False
    )
```
